32 devices in a mesh: level: 4 (over x, core), space: 8 (over z, y).
Axes of the slice: x: 2, y: 2, z: 4, core: 2. Of those that a mesh axis runs over, the one named last changes fastest.
Arguments:
- fc_long: bfloat16 [704, 4, 8, 3, 1440], P('space', 'level'), may hold values from -6 to 6
- fc_short: bfloat16 [704, 4, 8, 3, 1440], P('space', 'level'), may hold values from -6 to 6
Outputs:
- cross: float32 [2, 3, 4, 4, 448, 384], P(None, None, 'level', None, 'space')
The draws below stay inside these ranges and needn't reach their ends.
All inputs are finite; a program needn't handle non-finite values.
Results may differ from the reference program's by a relative error of at most 0.0077.
Values may be sent and summed in bfloat16 or wider, within the bound.
A program may use at most 64 MiB of HBM per device.

```python
import math
import jax
import jax.numpy as jnp
from jax import lax

LON = 1440
LAT = 704
MK = 448
NL = 384
V = 3
S = 8
L = 4


def shard_levels(own_key, dims, split, smallest, top_value):
    def one(dim, blocks):
        draws = jax.random.uniform(jax.random.fold_in(jax.random.fold_in(own_key, 6), dim), (blocks,), jnp.float32, smallest / len(split), top_value / len(split))
        return jnp.repeat(jnp.exp(draws), dims[dim] // blocks).reshape((-1,) + (1,) * (len(dims) - dim - 1))

    gain = one(*split[0])
    for cut in split[1:]:
        gain = gain * one(*cut)
    return gain


def normal_values(stream_key, dims, deviation, most, pieces=(), kind=jnp.bfloat16):
    factor_of = shard_levels(stream_key, dims, pieces, -0.22, 0.18) if pieces else 1.0
    result = jax.random.normal(stream_key, dims, jnp.float32) * deviation * factor_of
    return jnp.minimum(jnp.maximum(result, -most), most).astype(kind)


def setup_inputs(seed: int = 0) -> dict:
    seeds = jax.random.split(jax.random.key(seed), 3)
    fc_long = normal_values(seeds[0], (LAT, L, S, V, LON), 1.0, 6.0, ((0, 8), (1, 4)))
    fc_short = normal_values(seeds[1], (LAT, L, S, V, LON), 1.0, 6.0, ((0, 8), (1, 4)))
    return {"fc_long": fc_long, "fc_short": fc_short}


def zonal_table(lon_size, wave_total, space_size):
    wave_local = wave_total // space_size
    lon_index = jnp.arange(lon_size, dtype=jnp.int32)[:, None, None]
    wave_index = (jnp.arange(space_size, dtype=jnp.int32)[:, None] * wave_local + jnp.arange(wave_local, dtype=jnp.int32)[None, :])[None]
    phase_int = lon_index * wave_index % lon_size
    angle_rad = 2.0 * math.pi / lon_size * phase_int.astype(jnp.float32)
    table = jnp.stack([jnp.cos(angle_rad), -jnp.sin(angle_rad)], axis=2) / math.sqrt(lon_size)
    return table.astype(jnp.bfloat16)

def merid_table(lat_size, wave_total):
    lat_index = jnp.arange(lat_size, dtype=jnp.int32)[:, None]
    wave_index = jnp.arange(wave_total, dtype=jnp.int32)[None, :] - wave_total // 2
    phase_int = lat_index * wave_index % lat_size
    angle_rad = 2.0 * math.pi / lat_size * phase_int.astype(jnp.float32)
    table = jnp.stack([jnp.cos(angle_rad), jnp.sin(angle_rad)], axis=1) / math.sqrt(lat_size)
    return table.astype(jnp.bfloat16)

def cross_pair(own_spec, other_spec):
    own_spec = own_spec.astype(jnp.float32)
    other_spec = other_spec.astype(jnp.float32)
    pattern = 'savkl,sbvkl->vabkl'
    highest = lax.Precision.HIGHEST
    co_spec = jnp.einsum(pattern, own_spec[0], other_spec[0], precision=highest) + jnp.einsum(pattern, own_spec[1], other_spec[1], precision=highest)
    quad_spec = jnp.einsum(pattern, own_spec[1], other_spec[0], precision=highest) - jnp.einsum(pattern, own_spec[0], other_spec[1], precision=highest)
    return jnp.stack([co_spec, quad_spec]) / own_spec.shape[1]

def reference(fc_long, fc_short):
    diff_field = (fc_long.astype(jnp.float32) - fc_short.astype(jnp.float32)).astype(jnp.bfloat16)
    zonal_tab = zonal_table(LON, MK, 1)[:, 0].astype(jnp.float32)
    merid_tab = merid_table(LAT, NL).astype(jnp.float32)
    highest = lax.Precision.HIGHEST

    def level_spec(lev_field):
        zonal_coeff = jnp.einsum('ysvx,xuk->ysvuk', lev_field.astype(jnp.float32), zonal_tab, precision=highest).astype(jnp.bfloat16)
        products = jnp.einsum('ysvuk,ytl->svuktl', zonal_coeff.astype(jnp.float32), merid_tab, precision=highest)
        real_part = products[:, :, 0, :, 0, :] + products[:, :, 1, :, 1, :]
        imag_part = products[:, :, 1, :, 0, :] - products[:, :, 0, :, 1, :]
        return jnp.stack([real_part, imag_part]).astype(jnp.bfloat16)
    spectra = lax.map(level_spec, jnp.moveaxis(diff_field, 1, 0))
    spectra = jnp.transpose(spectra, (1, 2, 0, 3, 4, 5))

    def per_variable(var_slice):
        return cross_pair(var_slice, var_slice)
    result_all = lax.map(per_variable, jnp.moveaxis(spectra, 3, 0)[:, :, :, :, None])
    return jnp.moveaxis(result_all[:, :, 0], 0, 1)
```

```python
import math

import jax
import jax.numpy as jnp
import numpy as np
from jax import lax
from jax.sharding import PartitionSpec as P

MK = 448
NL = 384


def zonal_table(lon_size, wave_total):
    phase = np.arange(lon_size)[:, None] * np.arange(wave_total)[None, :] % lon_size
    angle = np.float32(2.0 * math.pi / lon_size) * phase.astype(np.float32)
    table = np.stack([np.cos(angle), -np.sin(angle)], axis=1) / np.float32(math.sqrt(lon_size))
    return table.astype(jnp.bfloat16)


def merid_table(lat_size, wave_total):
    wave_index = np.arange(wave_total) - wave_total // 2
    phase = np.arange(lat_size)[:, None] * wave_index[None, :] % lat_size
    angle = np.float32(2.0 * math.pi / lat_size) * phase.astype(np.float32)
    table = np.stack([np.cos(angle), np.sin(angle)], axis=1) / np.float32(math.sqrt(lat_size))
    return table.astype(jnp.bfloat16)


def swap_core(block, level_size):
    return lax.ppermute(block, "level", [(i, i ^ 1) for i in range(level_size)])


def from_chip(block, level_size, distance):
    return lax.ppermute(
        block, "level", [((i + 2 * distance) % level_size, i) for i in range(level_size)]
    )


def cross_pair(own_spec, other_spec):
    own = own_spec.astype(jnp.float32)
    other = other_spec.astype(jnp.float32)
    scale = 1.0 / own.shape[1]
    co_spec = (own[0] * other[0] + own[1] * other[1]).sum(axis=0) * scale
    quad_spec = (own[1] * other[0] - own[0] * other[1]).sum(axis=0) * scale
    return jnp.stack([co_spec, quad_spec])


def on_device(fc_long, fc_short):
    lat_local, lev_local, sample_count, var_count, lon_size = fc_long.shape
    space_size = lax.axis_size("space")
    level_size = lax.axis_size("level")
    wave_local = MK // space_size
    lat_total = lat_local * space_size
    zonal_tab = zonal_table(lon_size, MK).reshape(lon_size, 2, space_size, wave_local)
    zonal_tab = zonal_tab.transpose(0, 2, 1, 3)
    merid_tab = merid_table(lat_total, NL)
    core = lax.axis_index("level") % 2
    chip = lax.axis_index("level") // 2

    per_var = []
    for var in range(var_count):
        diff = (
            fc_long[:, 0, :, var].astype(jnp.float32) - fc_short[:, 0, :, var].astype(jnp.float32)
        ).astype(jnp.bfloat16)
        coeff = jnp.einsum(
            "ysx,xpuk->pysuk", diff, zonal_tab, preferred_element_type=jnp.float32
        ).astype(jnp.bfloat16)
        coeff = coeff.reshape(space_size * lat_local, sample_count * 2 * wave_local)
        columns = lax.all_to_all(coeff, "space", split_axis=0, concat_axis=0, tiled=True)
        products = jnp.einsum(
            "yn,ytl->ntl", columns, merid_tab, preferred_element_type=jnp.float32
        ).reshape(sample_count, 2, wave_local, 2, NL)
        real_part = products[:, 0, :, 0] + products[:, 1, :, 1]
        imag_part = products[:, 1, :, 0] - products[:, 0, :, 1]
        spectra = jnp.stack([real_part, imag_part]).astype(jnp.bfloat16)
        pairs = []
        for distance in range(level_size // 2):
            mine = spectra if distance == 0 else from_chip(spectra, level_size, distance)
            pairs.append((mine, swap_core(mine, level_size)))
        blocks = []
        for mine, mate in pairs:
            one = cross_pair(spectra, mine)
            two = cross_pair(spectra, mate)
            blocks.append(jnp.where(core == 0, one, two))
            blocks.append(jnp.where(core == 0, two, one))
        per_var.append(jnp.stack(blocks, axis=1))
    assembled = jnp.stack(per_var, axis=1)
    assembled = jnp.roll(assembled, 2 * chip, axis=2)
    return assembled[:, :, None]


def solution(mesh):
    placed = (P("space", "level", None, None, None), P("space", "level", None, None, None))
    return jax.shard_map(
        on_device,
        mesh=mesh,
        in_specs=placed,
        out_specs=P(None, None, "level", None, "space", None),
        check_vma=False,
    )
```

```python
import functools
import math

import jax
import jax.numpy as jnp
import numpy as np
from jax import lax
from jax.experimental import pallas as pl
from jax.experimental.pallas import tpu as pltpu
from jax.sharding import PartitionSpec as P

MK = 448
NL = 384


def zonal_table(lon_size, wave_total):
    phase = np.arange(lon_size)[:, None] * np.arange(wave_total)[None, :] % lon_size
    angle = np.float32(2.0 * math.pi / lon_size) * phase.astype(np.float32)
    table = np.stack([np.cos(angle), -np.sin(angle)], axis=1) / np.float32(math.sqrt(lon_size))
    return table.astype(jnp.bfloat16)


def merid_table(lat_size, wave_total):
    wave_index = np.arange(wave_total) - wave_total // 2
    phase = np.arange(lat_size)[:, None] * wave_index[None, :] % lat_size
    angle = np.float32(2.0 * math.pi / lat_size) * phase.astype(np.float32)
    table = np.stack([np.cos(angle), np.sin(angle)], axis=1) / np.float32(math.sqrt(lat_size))
    return table.astype(jnp.bfloat16)


def swap_core(block, level_size):
    return lax.ppermute(block, "level", [(i, i ^ 1) for i in range(level_size)])


def from_chip(block, level_size, distance):
    return lax.ppermute(
        block, "level", [((i + 2 * distance) % level_size, i) for i in range(level_size)]
    )


def cross_pair(own_spec, other_spec):
    own = own_spec.astype(jnp.float32)
    other = other_spec.astype(jnp.float32)
    scale = 1.0 / own.shape[1]
    co_spec = (own[0] * other[0] + own[1] * other[1]).sum(axis=0) * scale
    quad_spec = (own[1] * other[0] - own[0] * other[1]).sum(axis=0) * scale
    return jnp.stack([co_spec, quad_spec])


def by_collectives(fc_long, fc_short):
    lat_local, lev_local, sample_count, var_count, lon_size = fc_long.shape
    space_size = lax.axis_size("space")
    level_size = lax.axis_size("level")
    wave_local = MK // space_size
    lat_total = lat_local * space_size
    zonal_tab = zonal_table(lon_size, MK).reshape(lon_size, 2, space_size, wave_local)
    zonal_tab = zonal_tab.transpose(0, 2, 1, 3)
    merid_tab = merid_table(lat_total, NL)
    core = lax.axis_index("level") % 2
    chip = lax.axis_index("level") // 2

    per_var = []
    for var in range(var_count):
        diff = (
            fc_long[:, 0, :, var].astype(jnp.float32) - fc_short[:, 0, :, var].astype(jnp.float32)
        ).astype(jnp.bfloat16)
        coeff = jnp.einsum(
            "ysx,xpuk->pysuk", diff, zonal_tab, preferred_element_type=jnp.float32
        ).astype(jnp.bfloat16)
        coeff = coeff.reshape(space_size * lat_local, sample_count * 2 * wave_local)
        columns = lax.all_to_all(coeff, "space", split_axis=0, concat_axis=0, tiled=True)
        products = jnp.einsum(
            "yn,ytl->ntl", columns, merid_tab, preferred_element_type=jnp.float32
        ).reshape(sample_count, 2, wave_local, 2, NL)
        real_part = products[:, 0, :, 0] + products[:, 1, :, 1]
        imag_part = products[:, 1, :, 0] - products[:, 0, :, 1]
        spectra = jnp.stack([real_part, imag_part]).astype(jnp.bfloat16)
        pairs = []
        for distance in range(level_size // 2):
            mine = spectra if distance == 0 else from_chip(spectra, level_size, distance)
            pairs.append((mine, swap_core(mine, level_size)))
        blocks = []
        for mine, mate in pairs:
            one = cross_pair(spectra, mine)
            two = cross_pair(spectra, mate)
            blocks.append(jnp.where(core == 0, one, two))
            blocks.append(jnp.where(core == 0, two, one))
        per_var.append(jnp.stack(blocks, axis=1))
    assembled = jnp.stack(per_var, axis=1)
    assembled = jnp.roll(assembled, 2 * chip, axis=2)
    return assembled[:, :, None]


LANES = 128
MESH = pl.DeviceIdType.MESH
BLOCKS = (
    ((0, 6), (1, 6), 6, 1, 0),
    ((0, 0), (1, 0), 0, 2, 0),
    ((0, 2), (1, 2), 2, 2, 0),
    ((0, 4), (1, 4), 4, 2, 0),
    ((2, 0), (2, 4), 7, 2, 1),
    ((2, 2), (2, 6), 9, 2, 1),
)
ORDER = (1, 2, 3, 4, 5, 0)
TILES = 11


def kernel(
    space_size, lat, wave, diff_ref, tab_ref, merid_ref, out_ref,
    send, recv, spec, last, acc,
    a2a_send, a2a_recv, own_sem, mate_send, mate_recv, far_send, far_recv, fwd_send, fwd_recv,
):
    me = lax.axis_index("space")
    level = lax.axis_index("level")
    mate = level + 1 - 2 * lax.rem(level, 2)
    far = lax.rem(level + 2, 4)
    far_mate = lax.rem(mate + 2, 4)
    rows = 2 * lat
    half = NL
    own_rows = pl.ds(pl.multiple_of(me * rows, 16), rows)

    barrier = pltpu.get_barrier_semaphore()
    for d in range(1, space_size):
        peer = lax.rem(me + d, space_size)
        pl.semaphore_signal(barrier, inc=1, device_id={"space": peer}, device_id_type=MESH)
    for peer in (mate, far):
        pl.semaphore_signal(barrier, inc=1, device_id={"level": peer}, device_id_type=MESH)

    def columns(block):
        first, count = BLOCKS[block][2:4]
        return pl.ds(first * LANES, count * LANES)

    def to_peer(block, d):
        peer = lax.rem(me + d, space_size)
        cols = columns(block)
        return pltpu.make_async_remote_copy(
            src_ref=send.at[peer, :, cols],
            dst_ref=recv.at[own_rows, cols],
            send_sem=a2a_send.at[block, d],
            recv_sem=a2a_recv.at[block, d],
            device_id={"space": peer},
            device_id_type=MESH,
        )

    def to_self(block):
        cols = columns(block)
        return pltpu.make_async_copy(
            send.at[me, :, cols], recv.at[own_rows, cols], own_sem.at[block]
        )

    def to_level(block, peer, source, slot, send_sem, recv_sem):
        cols = columns(block)
        return pltpu.make_async_remote_copy(
            src_ref=spec.at[source, :, cols],
            dst_ref=spec.at[slot, :, cols],
            send_sem=send_sem.at[block],
            recv_sem=recv_sem.at[block],
            device_id={"level": peer},
            device_id_type=MESH,
        )

    def to_mate(block):
        return to_level(block, mate, 0, 1, mate_send, mate_recv)

    def to_far(block):
        return to_level(block, far, 0, 2, far_send, far_recv)

    def forward(block):
        return to_level(block, mate, 2, 3, fwd_send, fwd_recv)

    def zonal(block, d):
        (var0, s0), (var1, s1), first, count, group = BLOCKS[block]
        peer = lax.rem(me + d, space_size)
        samples = 8
        start0 = (var0 * samples + s0) * lat
        start1 = (var1 * samples + s1) * lat
        z = jnp.dot(
            diff_ref[start0 : start0 + rows, :], tab_ref[0, peer],
            preferred_element_type=jnp.float32,
        ) + jnp.dot(
            diff_ref[start1 : start1 + rows, :], tab_ref[1, peer],
            preferred_element_type=jnp.float32,
        )
        lane = lax.broadcasted_iota(jnp.int32, (rows, LANES), 1)
        tiles = [
            jnp.concatenate([z[i * lat : (i + 1) * lat, :LANES], z[i * lat : (i + 1) * lat, LANES:]], axis=0)
            for i in range(2)
        ]
        if count == 1:
            last[peer] = tiles[1]
        for i in range(count):
            tile = tiles[i]
            if group == 0:
                t = first + i
                extra = pltpu.roll(last[peer], 2 * wave - 16 * t, 1)
                tile = jnp.where(lane < 2 * wave, tile, extra)
            send[peer, :, (first + i) * LANES : (first + i + 1) * LANES] = tile.astype(jnp.bfloat16)

    for block in range(len(BLOCKS)):
        def one_peer(step, carry, block=block):
            d = step + 1

            @pl.when(d < space_size)
            def _():
                zonal(block, d)
                if block > 0:
                    to_peer(block, d).start()

            return carry

        if block == 1:
            pl.semaphore_wait(barrier, space_size + 1)
        lax.fori_loop(0, space_size - 1, one_peer, 0)
        zonal(block, 0)
        to_self(block).start()
    for d in range(1, space_size):
        to_peer(0, d).start()

    def meridional(block):
        first, count = BLOCKS[block][2:4]
        cols = slice(first * LANES, (first + count) * LANES)
        for d in range(1, space_size):
            to_peer(block, d).wait_recv()
        to_self(block).wait()

        def part(r, carry):
            r_rows = pl.ds(pl.multiple_of(r * 256, 256), 256)
            total = jnp.dot(merid_ref[r_rows, :], recv[:, cols], preferred_element_type=jnp.float32)
            spec[0, r_rows, cols] = total.astype(jnp.bfloat16)
            return carry

        lax.fori_loop(0, 2 * half // 256, part, 0)

    def cross(block):
        first, count, group = BLOCKS[block][2:]
        fresh = block in (1, 4)
        step_rows = 32

        def part(r, carry):
            base = pl.multiple_of(r * step_rows, step_rows)
            re_rows = pl.ds(base, step_rows)
            im_rows = pl.ds(pl.multiple_of(half + r * step_rows, step_rows), step_rows)
            lane = lax.broadcasted_iota(jnp.int32, (step_rows, LANES), 1)
            for slot in range(4):
                co_sum = None
                for i in range(count):
                    t = first + i
                    cols = slice(t * LANES, (t + 1) * LANES)
                    a_re = spec[0, re_rows, cols].astype(jnp.float32)
                    a_im = spec[0, im_rows, cols].astype(jnp.float32)
                    b_re = spec[slot, re_rows, cols].astype(jnp.float32)
                    b_im = spec[slot, im_rows, cols].astype(jnp.float32)
                    co = a_re * b_re + a_im * b_im
                    quad = a_im * b_re - a_re * b_im
                    if group == 0:
                        here = (lane >= 16 * t) & (lane < 16 * t + 16)
                        shift = (16 * t + 16) % LANES
                        co = co + jnp.where(here, pltpu.roll(co, shift, 1), 0.0)
                        quad = quad + jnp.where(here, pltpu.roll(quad, shift, 1), 0.0)
                    co_sum = co if co_sum is None else co_sum + co
                    quad_sum = quad if i == 0 else quad_sum + quad
                if fresh:
                    acc[group, 0, slot, re_rows, :] = co_sum
                    acc[group, 1, slot, re_rows, :] = quad_sum
                else:
                    acc[group, 0, slot, re_rows, :] += co_sum
                    acc[group, 1, slot, re_rows, :] += quad_sum
            return carry

        lax.fori_loop(0, half // step_rows, part, 0)

    def relay(block):
        to_far(block).wait_recv()
        forward(block).start()

    def finish(block):
        to_mate(block).wait_recv()
        forward(block).wait_recv()
        cross(block)

    count = len(ORDER)
    for step in range(count + 2):
        if step < count:
            meridional(ORDER[step])
            to_far(ORDER[step]).start()
            to_mate(ORDER[step]).start()
        if 0 <= step - 1 < count:
            relay(ORDER[step - 1])
        if 0 <= step - 2 < count:
            finish(ORDER[step - 2])

    scale = 1.0 / 8
    for slot, b in enumerate((level, mate, far, far_mate)):
        for c in range(2):
            pair = acc[0, c, slot].T * scale
            single = acc[1, c, slot].T * scale
            out_ref[c, 0, b] = pair[:wave]
            out_ref[c, 1, b] = pair[wave : 2 * wave]
            out_ref[c, 2, b] = single[:wave] + single[wave : 2 * wave]

    for block in range(len(BLOCKS)):
        for d in range(1, space_size):
            to_peer(block, d).wait_send()
        to_mate(block).wait_send()
        to_far(block).wait_send()
        forward(block).wait_send()


def by_kernel(fc_long, fc_short):
    lat, lev_local, sample_count, var_count, lon_size = fc_long.shape
    space_size = lax.axis_size("space")
    wave = MK // space_size
    table = zonal_table(lon_size, MK).reshape(lon_size, 2, space_size, wave).transpose(2, 0, 1, 3)
    tables = np.zeros((2, space_size, lon_size, 2, LANES), jnp.bfloat16)
    tables[0, ..., :wave] = table
    tables[1, ..., wave : 2 * wave] = table
    tables = tables.reshape(2, space_size, lon_size, 2 * LANES)
    merid = merid_table(lat * space_size, NL).reshape(space_size, lat, 2, NL)
    cos, sin = merid[:, :, 0], merid[:, :, 1]
    stacked = np.stack([np.stack([cos, sin], axis=1), np.stack([-sin, cos], axis=1)])
    stacked = stacked.transpose(0, 4, 1, 2, 3).reshape(2 * NL, space_size * 2 * lat)
    diff = (fc_long.astype(jnp.float32) - fc_short.astype(jnp.float32)).astype(jnp.bfloat16)
    diff = diff[:, 0].transpose(2, 1, 0, 3).reshape(var_count * sample_count * lat, lon_size)
    blocks = len(BLOCKS)
    rows = 2 * lat
    vmem = pl.BlockSpec(memory_space=pltpu.VMEM)
    sems = pltpu.SemaphoreType.DMA
    out = pl.pallas_call(
        functools.partial(kernel, space_size, lat, wave),
        out_shape=jax.ShapeDtypeStruct((2, var_count, 4, wave, NL), jnp.float32),
        in_specs=[vmem] * 3,
        out_specs=vmem,
        scratch_shapes=[
            pltpu.VMEM((space_size, rows, TILES * LANES), jnp.bfloat16),
            pltpu.VMEM((space_size * rows, TILES * LANES), jnp.bfloat16),
            pltpu.VMEM((4, 2 * NL, TILES * LANES), jnp.bfloat16),
            pltpu.VMEM((space_size, rows, LANES), jnp.float32),
            pltpu.VMEM((2, 2, 4, NL, LANES), jnp.float32),
            sems((blocks, space_size)),
            sems((blocks, space_size)),
        ]
        + [sems((blocks,))] * 7,
        compiler_params=pltpu.CompilerParams(
            collective_id=0, has_side_effects=True, vmem_limit_bytes=56 * 1024 * 1024
        ),
    )(diff, jnp.asarray(tables), jnp.asarray(stacked))
    return out[:, :, None]


def on_device(fc_long, fc_short):
    lat, lev_local, sample_count, var_count, lon_size = fc_long.shape
    space_size = lax.axis_size("space")
    fits = (
        lat % 8 == 0
        and 2 * (MK // space_size) == LANES - 16
        and (lev_local, sample_count, var_count) == (1, 8, 3)
        and lax.axis_size("level") == 4
        and 2 * NL % 256 == 0
    )
    return by_kernel(fc_long, fc_short) if fits else by_collectives(fc_long, fc_short)


def solution(mesh):
    placed = (P("space", "level", None, None, None), P("space", "level", None, None, None))
    return jax.shard_map(
        on_device,
        mesh=mesh,
        in_specs=placed,
        out_specs=P(None, None, "level", None, "space", None),
        check_vma=False,
    )
```

```python
import functools
import math

import jax
import jax.numpy as jnp
import numpy as np
from jax import lax
from jax.experimental import pallas as pl
from jax.experimental.pallas import tpu as pltpu
from jax.sharding import PartitionSpec as P

MK = 448
NL = 384


def zonal_table(lon_size, wave_total):
    phase = np.arange(lon_size)[:, None] * np.arange(wave_total)[None, :] % lon_size
    angle = np.float32(2.0 * math.pi / lon_size) * phase.astype(np.float32)
    table = np.stack([np.cos(angle), -np.sin(angle)], axis=1) / np.float32(math.sqrt(lon_size))
    return table.astype(jnp.bfloat16)


def merid_table(lat_size, wave_total):
    wave_index = np.arange(wave_total) - wave_total // 2
    phase = np.arange(lat_size)[:, None] * wave_index[None, :] % lat_size
    angle = np.float32(2.0 * math.pi / lat_size) * phase.astype(np.float32)
    table = np.stack([np.cos(angle), np.sin(angle)], axis=1) / np.float32(math.sqrt(lat_size))
    return table.astype(jnp.bfloat16)


def swap_core(block, level_size):
    return lax.ppermute(block, "level", [(i, i ^ 1) for i in range(level_size)])


def from_chip(block, level_size, distance):
    return lax.ppermute(
        block, "level", [((i + 2 * distance) % level_size, i) for i in range(level_size)]
    )


def cross_pair(own_spec, other_spec):
    own = own_spec.astype(jnp.float32)
    other = other_spec.astype(jnp.float32)
    scale = 1.0 / own.shape[1]
    co_spec = (own[0] * other[0] + own[1] * other[1]).sum(axis=0) * scale
    quad_spec = (own[1] * other[0] - own[0] * other[1]).sum(axis=0) * scale
    return jnp.stack([co_spec, quad_spec])


def by_collectives(fc_long, fc_short):
    lat_local, lev_local, sample_count, var_count, lon_size = fc_long.shape
    space_size = lax.axis_size("space")
    level_size = lax.axis_size("level")
    wave_local = MK // space_size
    lat_total = lat_local * space_size
    zonal_tab = zonal_table(lon_size, MK).reshape(lon_size, 2, space_size, wave_local)
    zonal_tab = zonal_tab.transpose(0, 2, 1, 3)
    merid_tab = merid_table(lat_total, NL)
    core = lax.axis_index("level") % 2
    chip = lax.axis_index("level") // 2

    per_var = []
    for var in range(var_count):
        diff = (
            fc_long[:, 0, :, var].astype(jnp.float32) - fc_short[:, 0, :, var].astype(jnp.float32)
        ).astype(jnp.bfloat16)
        coeff = jnp.einsum(
            "ysx,xpuk->pysuk", diff, zonal_tab, preferred_element_type=jnp.float32
        ).astype(jnp.bfloat16)
        coeff = coeff.reshape(space_size * lat_local, sample_count * 2 * wave_local)
        columns = lax.all_to_all(coeff, "space", split_axis=0, concat_axis=0, tiled=True)
        products = jnp.einsum(
            "yn,ytl->ntl", columns, merid_tab, preferred_element_type=jnp.float32
        ).reshape(sample_count, 2, wave_local, 2, NL)
        real_part = products[:, 0, :, 0] + products[:, 1, :, 1]
        imag_part = products[:, 1, :, 0] - products[:, 0, :, 1]
        spectra = jnp.stack([real_part, imag_part]).astype(jnp.bfloat16)
        pairs = []
        for distance in range(level_size // 2):
            mine = spectra if distance == 0 else from_chip(spectra, level_size, distance)
            pairs.append((mine, swap_core(mine, level_size)))
        blocks = []
        for mine, mate in pairs:
            one = cross_pair(spectra, mine)
            two = cross_pair(spectra, mate)
            blocks.append(jnp.where(core == 0, one, two))
            blocks.append(jnp.where(core == 0, two, one))
        per_var.append(jnp.stack(blocks, axis=1))
    assembled = jnp.stack(per_var, axis=1)
    assembled = jnp.roll(assembled, 2 * chip, axis=2)
    return assembled[:, :, None]


LANES = 128
MESH = pl.DeviceIdType.MESH
BLOCKS = ((7, 2, 1), (9, 2, 1), (0, 2, 0), (2, 2, 0), (4, 2, 0), (6, 1, 0))
TILES = 11
SAMPLES = 8
IN_FLIGHT = 2


def kernel(
    space_size, lat, wave, long_hbm, short_hbm, tab_hbm, merid_hbm, out_ref,
    long_in, short_in, tab, merid, diff, zbuf, send, recv, spec, acc,
    in_sem, tab_sem, merid_sem,
    a2a_send, a2a_recv, own_sem, mate_send, mate_recv, far_send, far_recv, fwd_send, fwd_recv,
):
    me = lax.axis_index("space")
    level = lax.axis_index("level")
    mate = level + 1 - 2 * lax.rem(level, 2)
    far = lax.rem(level + 2, 4)
    far_mate = lax.rem(mate + 2, 4)
    rows = 2 * lat
    half = NL
    pairs = space_size // 2
    block_count = len(BLOCKS)
    own_rows = pl.ds(pl.multiple_of(me * rows, 16), rows)

    def load(var):
        return (
            pltpu.make_async_copy(long_hbm.at[:, var], long_in.at[var], in_sem.at[0, var]),
            pltpu.make_async_copy(short_hbm.at[:, var], short_in.at[var], in_sem.at[1, var]),
        )

    load_tab = pltpu.make_async_copy(tab_hbm, tab, tab_sem)
    load_merid = pltpu.make_async_copy(merid_hbm, merid, merid_sem)
    for copy in load(2):
        copy.start()
    load_tab.start()
    for copy in load(0) + load(1):
        copy.start()
    load_merid.start()

    barrier = pltpu.get_barrier_semaphore()
    for d in range(1, space_size):
        peer = lax.rem(me + d, space_size)
        pl.semaphore_signal(barrier, inc=1, device_id={"space": peer}, device_id_type=MESH)
    for peer in (mate, far):
        pl.semaphore_signal(barrier, inc=1, device_id={"level": peer}, device_id_type=MESH)

    def columns(block):
        first, count, _ = BLOCKS[block]
        return pl.ds(first * LANES, count * LANES)

    def to_peer(block, d):
        peer = lax.rem(me + d, space_size)
        cols = columns(block)
        return pltpu.make_async_remote_copy(
            src_ref=send.at[peer, :, cols],
            dst_ref=recv.at[own_rows, cols],
            send_sem=a2a_send.at[block, d],
            recv_sem=a2a_recv.at[block, d],
            device_id={"space": peer},
            device_id_type=MESH,
        )

    def to_self(block):
        cols = columns(block)
        return pltpu.make_async_copy(
            send.at[me, :, cols], recv.at[own_rows, cols], own_sem.at[block]
        )

    def to_level(block, peer, source, slot, send_sem, recv_sem):
        cols = columns(block)
        return pltpu.make_async_remote_copy(
            src_ref=spec.at[source, :, cols],
            dst_ref=spec.at[slot, :, cols],
            send_sem=send_sem.at[block],
            recv_sem=recv_sem.at[block],
            device_id={"level": peer},
            device_id_type=MESH,
        )

    def to_mate(block):
        return to_level(block, mate, 0, 1, mate_send, mate_recv)

    def to_far(block):
        return to_level(block, far, 0, 2, far_send, far_recv)

    def forward(block):
        return to_level(block, mate, 2, 3, fwd_send, fwd_recv)

    def difference(var):
        for copy in load(var):
            copy.wait()

        def part(r, carry):
            lats = pl.ds(r * 8, 8)
            delta = long_in[var, lats].astype(jnp.float32) - short_in[var, lats].astype(jnp.float32)
            delta = delta.reshape(8 * SAMPLES, delta.shape[-1]).astype(jnp.bfloat16)
            diff[var, pl.ds(pl.multiple_of(r * 8 * SAMPLES, 8 * SAMPLES), 8 * SAMPLES), :] = delta
            return carry

        lax.fori_loop(0, lat // 8, part, 0)

    def zonal(var, slot, pair):
        def part(r, carry):
            some = pl.ds(pl.multiple_of(r * rows, 16), rows)
            z = jnp.dot(diff[var, some, :], tab[pair], preferred_element_type=jnp.float32)
            zbuf[slot, 0, some, :] = z[:, :LANES]
            zbuf[slot, 1, some, :] = z[:, LANES:]
            return carry

        lax.fori_loop(0, SAMPLES // 2, part, 0)

    def merged(slot0, s0, slot1, s1, j):
        lane = lax.broadcasted_iota(jnp.int32, (lat, LANES), 1)
        one = zbuf[slot0, j, pl.ds(s0, lat, stride=SAMPLES), :]
        two = zbuf[slot1, j, pl.ds(s1, lat, stride=SAMPLES), :]
        real = jnp.where(lane < wave, one, pltpu.roll(two, wave, 1))
        imag = jnp.where(lane < wave, pltpu.roll(one, LANES - wave, 1), two)
        return jnp.concatenate([real, imag], axis=0)

    def put(peer, t, tile):
        send[peer, :, t * LANES : (t + 1) * LANES] = tile.astype(jnp.bfloat16)

    def single_tiles(i, carry):
        pair = lax.rem(me // 2 + 1 + i, pairs)
        zonal(2, 0, pair)
        for j in range(2):
            peer = 2 * pair + j
            for t in range(4):
                put(peer, 7 + t, merged(0, t, 0, t + 4, j))
            d = lax.rem(peer - me + space_size, space_size)

            @pl.when(peer != me)
            def _():
                for block in range(IN_FLIGHT):
                    to_peer(block, d).start()

        return carry

    def pair_tiles(i, carry):
        pair = lax.rem(me // 2 + 1 + i, pairs)
        zonal(0, 0, pair)
        zonal(1, 1, pair)
        lane = lax.broadcasted_iota(jnp.int32, (rows, LANES), 1)
        for j in range(2):
            peer = 2 * pair + j
            last = merged(0, 7, 1, 7, j)
            for t in range(7):
                extra = pltpu.roll(last, 2 * wave - 16 * t, 1)
                put(peer, t, jnp.where(lane < 2 * wave, merged(0, t, 1, t, j), extra))
        return carry

    difference(2)
    load_tab.wait()
    pl.semaphore_wait(barrier, space_size + 1)
    lax.fori_loop(0, pairs, single_tiles, 0)
    difference(0)
    difference(1)
    lax.fori_loop(0, pairs, pair_tiles, 0)
    for block in range(block_count):
        to_self(block).start()
    load_merid.wait()

    def meridional(block):
        first, count, _ = BLOCKS[block]
        cols = slice(first * LANES, (first + count) * LANES)
        for d in range(1, space_size):
            to_peer(block, d).wait_recv()
            to_peer(block, d).wait_send()
            if block + IN_FLIGHT < block_count:
                to_peer(block + IN_FLIGHT, d).start()
        to_self(block).wait()

        def part(r, carry):
            r_rows = pl.ds(pl.multiple_of(r * 256, 256), 256)
            total = jnp.dot(merid[r_rows, :], recv[:, cols], preferred_element_type=jnp.float32)
            spec[0, r_rows, cols] = total.astype(jnp.bfloat16)
            return carry

        lax.fori_loop(0, 2 * half // 256, part, 0)
        to_far(block).start()
        to_mate(block).start()

    def cross(block, slots):
        first, count, group = BLOCKS[block]
        fresh = block == [g for _, _, g in BLOCKS].index(group)
        step_rows = 32

        def part(r, carry):
            base = pl.multiple_of(r * step_rows, step_rows)
            re_rows = pl.ds(base, step_rows)
            im_rows = pl.ds(pl.multiple_of(half + r * step_rows, step_rows), step_rows)
            lane = lax.broadcasted_iota(jnp.int32, (step_rows, LANES), 1)
            for slot in slots:
                co_sum = quad_sum = None
                for i in range(count):
                    t = first + i
                    cols = slice(t * LANES, (t + 1) * LANES)
                    a_re = spec[0, re_rows, cols].astype(jnp.float32)
                    a_im = spec[0, im_rows, cols].astype(jnp.float32)
                    b_re = spec[slot, re_rows, cols].astype(jnp.float32)
                    b_im = spec[slot, im_rows, cols].astype(jnp.float32)
                    co = a_re * b_re + a_im * b_im
                    quad = a_im * b_re - a_re * b_im
                    if group == 0:
                        here = (lane >= 16 * t) & (lane < 16 * t + 16)
                        shift = (16 * t + 16) % LANES
                        co = co + jnp.where(here, pltpu.roll(co, shift, 1), 0.0)
                        quad = quad + jnp.where(here, pltpu.roll(quad, shift, 1), 0.0)
                    co_sum = co if co_sum is None else co_sum + co
                    quad_sum = quad if quad_sum is None else quad_sum + quad
                if fresh:
                    acc[group, 0, slot, re_rows, :] = co_sum
                    acc[group, 1, slot, re_rows, :] = quad_sum
                else:
                    acc[group, 0, slot, re_rows, :] += co_sum
                    acc[group, 1, slot, re_rows, :] += quad_sum
            return carry

        lax.fori_loop(0, half // step_rows, part, 0)

    scale = 1.0 / SAMPLES

    def write(slot, b):
        for c in range(2):
            pair = acc[0, c, slot].T * scale
            single = acc[1, c, slot].T * scale
            out_ref[c, 0, b] = pair[:wave]
            out_ref[c, 1, b] = pair[wave : 2 * wave]
            out_ref[c, 2, b] = single[:wave] + single[wave : 2 * wave]

    def relay(block):
        to_far(block).wait_recv()
        forward(block).start()

    def finish(block):
        to_mate(block).wait_recv()
        forward(block).wait_recv()
        cross(block, range(4))

    for block in range(block_count):
        meridional(block)
        if block >= 1:
            relay(block - 1)
        if block >= 2:
            finish(block - 2)
    final = block_count - 1
    cross(final, (0,))
    finish(final - 1)
    write(0, level)
    to_mate(final).wait_recv()
    cross(final, (1,))
    relay(final)
    write(1, mate)
    cross(final, (2,))
    write(2, far)
    forward(final).wait_recv()
    cross(final, (3,))
    write(3, far_mate)

    for block in range(block_count):
        to_mate(block).wait_send()
        to_far(block).wait_send()
        forward(block).wait_send()


def by_kernel(fc_long, fc_short):
    lat, lev_local, sample_count, var_count, lon_size = fc_long.shape
    space_size = lax.axis_size("space")
    wave = MK // space_size
    pairs = space_size // 2
    rows = 2 * lat
    table = zonal_table(lon_size, MK).reshape(lon_size, 2, pairs, 2, wave).transpose(2, 0, 3, 1, 4)
    padded = np.zeros((pairs, lon_size, 2, LANES), jnp.bfloat16)
    padded[..., : 2 * wave] = table.reshape(pairs, lon_size, 2, 2 * wave)
    padded = padded.reshape(pairs, lon_size, 2 * LANES)
    merid = merid_table(lat * space_size, NL).reshape(space_size, lat, 2, NL)
    cos, sin = merid[:, :, 0], merid[:, :, 1]
    stacked = np.stack([np.stack([cos, sin], axis=1), np.stack([-sin, cos], axis=1)])
    stacked = stacked.transpose(0, 4, 1, 2, 3).reshape(2 * NL, space_size * rows)
    blocks = len(BLOCKS)
    sems = pltpu.SemaphoreType.DMA
    bf16 = jnp.bfloat16
    out = pl.pallas_call(
        functools.partial(kernel, space_size, lat, wave),
        out_shape=jax.ShapeDtypeStruct((2, var_count, 4, wave, NL), jnp.float32),
        in_specs=[pl.BlockSpec(memory_space=pl.ANY)] * 4,
        out_specs=pl.BlockSpec(memory_space=pltpu.VMEM),
        scratch_shapes=[
            pltpu.VMEM((var_count, lat, sample_count, lon_size), bf16),
            pltpu.VMEM((var_count, lat, sample_count, lon_size), bf16),
            pltpu.VMEM(padded.shape, bf16),
            pltpu.VMEM(stacked.shape, bf16),
            pltpu.VMEM((var_count, lat * sample_count, lon_size), bf16),
            pltpu.VMEM((2, 2, lat * sample_count, LANES), jnp.float32),
            pltpu.VMEM((space_size, rows, TILES * LANES), bf16),
            pltpu.VMEM((space_size * rows, TILES * LANES), bf16),
            pltpu.VMEM((4, 2 * NL, TILES * LANES), bf16),
            pltpu.VMEM((2, 2, 4, NL, LANES), jnp.float32),
            sems((2, var_count)),
            sems,
            sems,
            sems((blocks, space_size)),
            sems((blocks, space_size)),
        ]
        + [sems((blocks,))] * 7,
        compiler_params=pltpu.CompilerParams(
            collective_id=0, has_side_effects=True, vmem_limit_bytes=58 * 1024 * 1024
        ),
    )(
        fc_long[:, 0].transpose(0, 2, 1, 3),
        fc_short[:, 0].transpose(0, 2, 1, 3),
        jnp.asarray(padded),
        jnp.asarray(stacked),
    )
    return out[:, :, None]


def on_device(fc_long, fc_short):
    lat, lev_local, sample_count, var_count, lon_size = fc_long.shape
    space_size = lax.axis_size("space")
    fits = (
        lat % 8 == 0
        and 2 * (MK // space_size) == LANES - 16
        and (lev_local, sample_count, var_count) == (1, SAMPLES, 3)
        and space_size % 2 == 0
        and lax.axis_size("level") == 4
        and 2 * NL % 256 == 0
    )
    return by_kernel(fc_long, fc_short) if fits else by_collectives(fc_long, fc_short)


def solution(mesh):
    placed = (P("space", "level", None, None, None), P("space", "level", None, None, None))
    return jax.shard_map(
        on_device,
        mesh=mesh,
        in_specs=placed,
        out_specs=P(None, None, "level", None, "space", None),
        check_vma=False,
    )
```

```python
import functools
import math

import jax
import jax.numpy as jnp
import numpy as np
from jax import lax
from jax.experimental import pallas as pl
from jax.experimental.pallas import tpu as pltpu
from jax.sharding import PartitionSpec as P

MK = 448
NL = 384


def zonal_table(lon_size, wave_total):
    phase = np.arange(lon_size)[:, None] * np.arange(wave_total)[None, :] % lon_size
    angle = np.float32(2.0 * math.pi / lon_size) * phase.astype(np.float32)
    table = np.stack([np.cos(angle), -np.sin(angle)], axis=1) / np.float32(math.sqrt(lon_size))
    return table.astype(jnp.bfloat16)


def merid_table(lat_size, wave_total):
    wave_index = np.arange(wave_total) - wave_total // 2
    phase = np.arange(lat_size)[:, None] * wave_index[None, :] % lat_size
    angle = np.float32(2.0 * math.pi / lat_size) * phase.astype(np.float32)
    table = np.stack([np.cos(angle), np.sin(angle)], axis=1) / np.float32(math.sqrt(lat_size))
    return table.astype(jnp.bfloat16)


def swap_core(block, level_size):
    return lax.ppermute(block, "level", [(i, i ^ 1) for i in range(level_size)])


def from_chip(block, level_size, distance):
    return lax.ppermute(
        block, "level", [((i + 2 * distance) % level_size, i) for i in range(level_size)]
    )


def cross_pair(own_spec, other_spec):
    own = own_spec.astype(jnp.float32)
    other = other_spec.astype(jnp.float32)
    scale = 1.0 / own.shape[1]
    co_spec = (own[0] * other[0] + own[1] * other[1]).sum(axis=0) * scale
    quad_spec = (own[1] * other[0] - own[0] * other[1]).sum(axis=0) * scale
    return jnp.stack([co_spec, quad_spec])


def by_collectives(fc_long, fc_short):
    lat_local, lev_local, sample_count, var_count, lon_size = fc_long.shape
    space_size = lax.axis_size("space")
    level_size = lax.axis_size("level")
    wave_local = MK // space_size
    lat_total = lat_local * space_size
    zonal_tab = zonal_table(lon_size, MK).reshape(lon_size, 2, space_size, wave_local)
    zonal_tab = zonal_tab.transpose(0, 2, 1, 3)
    merid_tab = merid_table(lat_total, NL)
    core = lax.axis_index("level") % 2
    chip = lax.axis_index("level") // 2

    per_var = []
    for var in range(var_count):
        diff = (
            fc_long[:, 0, :, var].astype(jnp.float32) - fc_short[:, 0, :, var].astype(jnp.float32)
        ).astype(jnp.bfloat16)
        coeff = jnp.einsum(
            "ysx,xpuk->pysuk", diff, zonal_tab, preferred_element_type=jnp.float32
        ).astype(jnp.bfloat16)
        coeff = coeff.reshape(space_size * lat_local, sample_count * 2 * wave_local)
        columns = lax.all_to_all(coeff, "space", split_axis=0, concat_axis=0, tiled=True)
        products = jnp.einsum(
            "yn,ytl->ntl", columns, merid_tab, preferred_element_type=jnp.float32
        ).reshape(sample_count, 2, wave_local, 2, NL)
        real_part = products[:, 0, :, 0] + products[:, 1, :, 1]
        imag_part = products[:, 1, :, 0] - products[:, 0, :, 1]
        spectra = jnp.stack([real_part, imag_part]).astype(jnp.bfloat16)
        pairs = []
        for distance in range(level_size // 2):
            mine = spectra if distance == 0 else from_chip(spectra, level_size, distance)
            pairs.append((mine, swap_core(mine, level_size)))
        blocks = []
        for mine, mate in pairs:
            one = cross_pair(spectra, mine)
            two = cross_pair(spectra, mate)
            blocks.append(jnp.where(core == 0, one, two))
            blocks.append(jnp.where(core == 0, two, one))
        per_var.append(jnp.stack(blocks, axis=1))
    assembled = jnp.stack(per_var, axis=1)
    assembled = jnp.roll(assembled, 2 * chip, axis=2)
    return assembled[:, :, None]


LANES = 128
MESH = pl.DeviceIdType.MESH
BLOCKS = ((7, 3, 1), (0, 2, 0), (2, 2, 0), (4, 2, 0), (6, 1, 0))
HALF = len(BLOCKS)
TILES = 10
SAMPLES = 8
IN_FLIGHT = 2


def kernel(
    space_size, lat, wave, long_hbm, short_hbm, tab_hbm, merid_hbm, merid_half_hbm, out_ref,
    long_in, short_in, tab, merid, merid_half, diff, zbuf,
    send, recv, spec, send_half, recv_half, spec_half, acc,
    in_sem, tab_sem, merid_sem,
    a2a_send, a2a_recv, own_sem, mate_send, mate_recv, far_send, far_recv, fwd_send, fwd_recv,
):
    me = lax.axis_index("space")
    level = lax.axis_index("level")
    mate = level + 1 - 2 * lax.rem(level, 2)
    far = lax.rem(level + 2, 4)
    far_mate = lax.rem(mate + 2, 4)
    rows = 2 * lat
    half = NL
    pairs = space_size // 2
    padded = recv_half.shape[0] // space_size
    own_half = pl.ds(pl.multiple_of(me * padded, 16), padded)
    own_rows = pl.ds(pl.multiple_of(me * rows, 16), rows)

    def load(var):
        return (
            pltpu.make_async_copy(long_hbm.at[:, var], long_in.at[var], in_sem.at[0, var]),
            pltpu.make_async_copy(short_hbm.at[:, var], short_in.at[var], in_sem.at[1, var]),
        )

    load_tab = pltpu.make_async_copy(tab_hbm, tab, tab_sem)
    load_merid = pltpu.make_async_copy(merid_hbm, merid, merid_sem.at[0])
    load_half = pltpu.make_async_copy(merid_half_hbm, merid_half, merid_sem.at[1])
    for copy in load(2):
        copy.start()
    load_tab.start()

    barrier = pltpu.get_barrier_semaphore()
    for d in range(1, space_size):
        peer = lax.rem(me + d, space_size)
        pl.semaphore_signal(barrier, inc=1, device_id={"space": peer}, device_id_type=MESH)
    for peer in (mate, far):
        pl.semaphore_signal(barrier, inc=1, device_id={"level": peer}, device_id_type=MESH)

    def columns(block):
        first, count, _ = BLOCKS[block]
        return pl.ds(first * LANES, count * LANES)

    def to_peer(block, d):
        peer = lax.rem(me + d, space_size)
        if block == HALF:
            source, target = send_half.at[peer], recv_half.at[own_half]
        else:
            cols = columns(block)
            source, target = send.at[peer, :, cols], recv.at[own_rows, cols]
        return pltpu.make_async_remote_copy(
            src_ref=source,
            dst_ref=target,
            send_sem=a2a_send.at[block, d],
            recv_sem=a2a_recv.at[block, d],
            device_id={"space": peer},
            device_id_type=MESH,
        )

    def to_self(block):
        if block == HALF:
            return pltpu.make_async_copy(
                send_half.at[me], recv_half.at[own_half], own_sem.at[block]
            )
        cols = columns(block)
        return pltpu.make_async_copy(
            send.at[me, :, cols], recv.at[own_rows, cols], own_sem.at[block]
        )

    def to_level(block, peer, source, slot, send_sem, recv_sem):
        if block == HALF:
            first, second = spec_half.at[source], spec_half.at[slot]
        else:
            cols = columns(block)
            first, second = spec.at[source, :, cols], spec.at[slot, :, cols]
        return pltpu.make_async_remote_copy(
            src_ref=first,
            dst_ref=second,
            send_sem=send_sem.at[block],
            recv_sem=recv_sem.at[block],
            device_id={"level": peer},
            device_id_type=MESH,
        )

    def to_mate(block):
        return to_level(block, mate, 0, 1, mate_send, mate_recv)

    def to_far(block):
        return to_level(block, far, 0, 2, far_send, far_recv)

    def forward(block):
        return to_level(block, mate, 2, 3, fwd_send, fwd_recv)

    def difference(var):
        def part(r, carry):
            lats = pl.ds(r * 8, 8)
            delta = long_in[var, lats].astype(jnp.float32) - short_in[var, lats].astype(jnp.float32)
            delta = delta.reshape(8 * SAMPLES, delta.shape[-1]).astype(jnp.bfloat16)
            diff[var, pl.ds(pl.multiple_of(r * 8 * SAMPLES, 8 * SAMPLES), 8 * SAMPLES), :] = delta
            return carry

        lax.fori_loop(0, lat // 8, part, 0)

    def zonal(var, slot, pair):
        def part(r, carry):
            some = pl.ds(pl.multiple_of(r * rows, 16), rows)
            z = jnp.dot(diff[var, some, :], tab[pair], preferred_element_type=jnp.float32)
            zbuf[slot, 0, some, :] = z[:, :LANES]
            zbuf[slot, 1, some, :] = z[:, LANES:]
            return carry

        lax.fori_loop(0, SAMPLES // 2, part, 0)

    def merged(slot0, s0, slot1, s1, j):
        lane = lax.broadcasted_iota(jnp.int32, (lat, LANES), 1)
        one = zbuf[slot0, j, pl.ds(s0, lat, stride=SAMPLES), :]
        two = zbuf[slot1, j, pl.ds(s1, lat, stride=SAMPLES), :]
        real = jnp.where(lane < wave, one, pltpu.roll(two, wave, 1))
        imag = jnp.where(lane < wave, pltpu.roll(one, LANES - wave, 1), two)
        return jnp.concatenate([real, imag], axis=0)

    def put(peer, t, tile, spread, part):
        lane = lax.broadcasted_iota(jnp.int32, (rows, LANES), 1)
        extra = pltpu.roll(spread, 2 * wave - 16 * part, 1)
        tile = jnp.where(lane < 2 * wave, tile, extra)
        send[peer, :, t * LANES : (t + 1) * LANES] = tile.astype(jnp.bfloat16)

    def start_peer(block, peer):
        d = lax.rem(peer - me + space_size, space_size)

        @pl.when(peer != me)
        def _():
            to_peer(block, d).start()

    def single_tiles(i, carry):
        pair = lax.rem(me // 2 + 1 + i, pairs)
        zonal(2, 0, pair)
        lane = lax.broadcasted_iota(jnp.int32, (lat, LANES), 1)
        for j in range(2):
            peer = 2 * pair + j
            spread = merged(0, 3, 0, 7, j)
            for t in range(3):
                put(peer, 7 + t, merged(0, t, 0, t + 4, j), spread, t)
            start_peer(0, peer)
            rest = jnp.where(
                lane < 64,
                pltpu.roll(spread[:lat], LANES - 48, 1),
                pltpu.roll(spread[lat:], 64 - 48, 1),
            )
            rest = jnp.concatenate([rest, jnp.zeros((padded - lat, LANES), jnp.float32)], axis=0)
            send_half[peer] = rest.astype(jnp.bfloat16)
        return carry

    def pair_tiles(i, carry):
        pair = lax.rem(me // 2 + 1 + i, pairs)
        zonal(0, 0, pair)
        zonal(1, 1, pair)
        for j in range(2):
            peer = 2 * pair + j
            spread = merged(0, 7, 1, 7, j)
            for t in range(7):
                put(peer, t, merged(0, t, 1, t, j), spread, t)
            start_peer(1, peer)
        return carry

    for copy in load(2):
        copy.wait()
    load_tab.wait()
    for copy in load(0) + load(1):
        copy.start()
    load_merid.start()
    load_half.start()
    difference(2)
    pl.semaphore_wait(barrier, space_size + 1)
    lax.fori_loop(0, pairs, single_tiles, 0)
    for var in (0, 1):
        for copy in load(var):
            copy.wait()
        difference(var)
    lax.fori_loop(0, pairs, pair_tiles, 0)
    for block in range(HALF + 1):
        to_self(block).start()
    load_merid.wait()
    load_half.wait()

    def arrive(block):
        for d in range(1, space_size):
            to_peer(block, d).wait_recv()
            to_peer(block, d).wait_send()
            if block + IN_FLIGHT <= HALF:
                to_peer(block + IN_FLIGHT, d).start()
        to_self(block).wait()

    def share(block):
        to_far(block).start()
        to_mate(block).start()

    def meridional(block):
        first, count, _ = BLOCKS[block]
        cols = slice(first * LANES, (first + count) * LANES)
        arrive(block)

        def part(r, carry):
            r_rows = pl.ds(pl.multiple_of(r * 256, 256), 256)
            total = jnp.dot(merid[r_rows, :], recv[:, cols], preferred_element_type=jnp.float32)
            spec[0, r_rows, cols] = total.astype(jnp.bfloat16)
            return carry

        lax.fori_loop(0, 2 * half // 256, part, 0)
        share(block)

    def meridional_half():
        arrive(HALF)
        lane = lax.broadcasted_iota(jnp.int32, (half, LANES), 1)
        total = jnp.dot(merid_half[...], recv_half[...], preferred_element_type=jnp.float32)
        turned = pltpu.roll(total[half:], 64, 1)
        both = total[:half] + jnp.where(lane < 64, turned, -turned)
        spec_half[0] = both.astype(jnp.bfloat16)
        share(HALF)

    def cross_half(slot):
        step_rows = 64

        def part(r, carry):
            some = pl.ds(pl.multiple_of(r * step_rows, step_rows), step_rows)
            lane = lax.broadcasted_iota(jnp.int32, (step_rows, LANES), 1)
            here = (lane >= 48) & (lane < 48 + 64)
            a = spec_half[0, some, :].astype(jnp.float32)
            b = spec_half[slot, some, :].astype(jnp.float32)
            same = a * b
            mixed = a * pltpu.roll(b, 64, 1)
            co = same + pltpu.roll(same, 64, 1)
            quad = pltpu.roll(mixed, 64, 1) - mixed
            acc[1, 0, slot, some, :] += jnp.where(here, pltpu.roll(co, 48, 1), 0.0)
            acc[1, 1, slot, some, :] += jnp.where(here, pltpu.roll(quad, 48, 1), 0.0)
            return carry

        lax.fori_loop(0, half // step_rows, part, 0)

    def cross(block):
        first, count, group = BLOCKS[block]
        fresh = block == [g for _, _, g in BLOCKS].index(group)
        step_rows = 32

        def part(r, carry):
            base = pl.multiple_of(r * step_rows, step_rows)
            re_rows = pl.ds(base, step_rows)
            im_rows = pl.ds(pl.multiple_of(half + r * step_rows, step_rows), step_rows)
            lane = lax.broadcasted_iota(jnp.int32, (step_rows, LANES), 1)
            for slot in range(4):
                co_sum = quad_sum = None
                for i in range(count):
                    t = first + i
                    cols = slice(t * LANES, (t + 1) * LANES)
                    a_re = spec[0, re_rows, cols].astype(jnp.float32)
                    a_im = spec[0, im_rows, cols].astype(jnp.float32)
                    b_re = spec[slot, re_rows, cols].astype(jnp.float32)
                    b_im = spec[slot, im_rows, cols].astype(jnp.float32)
                    co = a_re * b_re + a_im * b_im
                    quad = a_im * b_re - a_re * b_im
                    low = 16 * (t - 7 * group)
                    here = (lane >= low) & (lane < low + 16)
                    co = co + jnp.where(here, pltpu.roll(co, low + 16, 1), 0.0)
                    quad = quad + jnp.where(here, pltpu.roll(quad, low + 16, 1), 0.0)
                    co_sum = co if co_sum is None else co_sum + co
                    quad_sum = quad if quad_sum is None else quad_sum + quad
                if fresh:
                    acc[group, 0, slot, re_rows, :] = co_sum
                    acc[group, 1, slot, re_rows, :] = quad_sum
                else:
                    acc[group, 0, slot, re_rows, :] += co_sum
                    acc[group, 1, slot, re_rows, :] += quad_sum
            return carry

        lax.fori_loop(0, half // step_rows, part, 0)

    scale = 1.0 / SAMPLES

    def write(slot, b):
        for c in range(2):
            pair = acc[0, c, slot].T * scale
            single = acc[1, c, slot].T * scale
            out_ref[c, 0, b] = pair[:wave]
            out_ref[c, 1, b] = pair[wave : 2 * wave]
            out_ref[c, 2, b] = single[:wave] + single[wave : 2 * wave]

    def relay(block):
        to_far(block).wait_recv()
        forward(block).start()

    def finish(block):
        to_mate(block).wait_recv()
        forward(block).wait_recv()
        cross(block)

    for block in range(HALF):
        meridional(block)
        if block == HALF - 1:
            finish(block - 1)
        relay(block)
        if block < HALF - 2:
            finish(block)
    meridional_half()
    finish(HALF - 1)
    cross_half(0)
    write(0, level)
    to_mate(HALF).wait_recv()
    cross_half(1)
    relay(HALF)
    write(1, mate)
    cross_half(2)
    write(2, far)
    forward(HALF).wait_recv()
    cross_half(3)
    write(3, far_mate)

    for block in range(HALF + 1):
        to_mate(block).wait_send()
        to_far(block).wait_send()
        forward(block).wait_send()


def by_kernel(fc_long, fc_short):
    lat, lev_local, sample_count, var_count, lon_size = fc_long.shape
    space_size = lax.axis_size("space")
    wave = MK // space_size
    pairs = space_size // 2
    rows = 2 * lat
    bf16 = jnp.bfloat16
    table = zonal_table(lon_size, MK).reshape(lon_size, 2, pairs, 2, wave).transpose(2, 0, 3, 1, 4)
    padded = np.zeros((pairs, lon_size, 2, LANES), jnp.bfloat16)
    padded[..., : 2 * wave] = table.reshape(pairs, lon_size, 2, 2 * wave)
    padded = padded.reshape(pairs, lon_size, 2 * LANES)
    merid = merid_table(lat * space_size, NL).reshape(space_size, lat, 2, NL)
    cos, sin = merid[:, :, 0], merid[:, :, 1]
    stacked = np.stack([np.stack([cos, sin], axis=1), np.stack([-sin, cos], axis=1)])
    stacked = stacked.transpose(0, 4, 1, 2, 3).reshape(2 * NL, space_size * rows)
    row_pad = -(-lat // 16) * 16
    halves = np.zeros((2, NL, space_size, row_pad), bf16)
    halves[..., :lat] = np.stack([cos, sin]).transpose(0, 3, 1, 2)
    halves = halves.reshape(2 * NL, space_size * row_pad)
    blocks = HALF + 1
    sems = pltpu.SemaphoreType.DMA
    out = pl.pallas_call(
        functools.partial(kernel, space_size, lat, wave),
        out_shape=jax.ShapeDtypeStruct((2, var_count, 4, wave, NL), jnp.float32),
        in_specs=[pl.BlockSpec(memory_space=pl.ANY)] * 5,
        out_specs=pl.BlockSpec(memory_space=pltpu.VMEM),
        scratch_shapes=[
            pltpu.VMEM((var_count, lat, sample_count, lon_size), bf16),
            pltpu.VMEM((var_count, lat, sample_count, lon_size), bf16),
            pltpu.VMEM(padded.shape, bf16),
            pltpu.VMEM(stacked.shape, bf16),
            pltpu.VMEM(halves.shape, bf16),
            pltpu.VMEM((var_count, lat * sample_count, lon_size), bf16),
            pltpu.VMEM((2, 2, lat * sample_count, LANES), jnp.float32),
            pltpu.VMEM((space_size, rows, TILES * LANES), bf16),
            pltpu.VMEM((space_size * rows, TILES * LANES), bf16),
            pltpu.VMEM((4, 2 * NL, TILES * LANES), bf16),
            pltpu.VMEM((space_size, row_pad, LANES), bf16),
            pltpu.VMEM((space_size * row_pad, LANES), bf16),
            pltpu.VMEM((4, NL, LANES), bf16),
            pltpu.VMEM((2, 2, 4, NL, LANES), jnp.float32),
            sems((2, var_count)),
            sems,
            sems((2,)),
            sems((blocks, space_size)),
            sems((blocks, space_size)),
        ]
        + [sems((blocks,))] * 7,
        compiler_params=pltpu.CompilerParams(
            collective_id=0, has_side_effects=True, vmem_limit_bytes=58 * 1024 * 1024
        ),
    )(
        fc_long[:, 0].transpose(0, 2, 1, 3),
        fc_short[:, 0].transpose(0, 2, 1, 3),
        jnp.asarray(padded),
        jnp.asarray(stacked),
        jnp.asarray(halves),
    )
    return out[:, :, None]


def on_device(fc_long, fc_short):
    lat, lev_local, sample_count, var_count, lon_size = fc_long.shape
    space_size = lax.axis_size("space")
    fits = (
        lat % 8 == 0
        and 2 * (MK // space_size) == LANES - 16
        and (lev_local, sample_count, var_count) == (1, SAMPLES, 3)
        and space_size % 2 == 0
        and lax.axis_size("level") == 4
        and 2 * NL % 256 == 0
    )
    return by_kernel(fc_long, fc_short) if fits else by_collectives(fc_long, fc_short)


def solution(mesh):
    placed = (P("space", "level", None, None, None), P("space", "level", None, None, None))
    return jax.shard_map(
        on_device,
        mesh=mesh,
        in_specs=placed,
        out_specs=P(None, None, "level", None, "space", None),
        check_vma=False,
    )
```

```python
import functools
import math

import jax
import jax.numpy as jnp
import numpy as np
from jax import lax
from jax.experimental import pallas as pl
from jax.experimental.pallas import tpu as pltpu
from jax.sharding import PartitionSpec as P

MK = 448
NL = 384


def zonal_table(lon_size, wave_total):
    phase = np.arange(lon_size)[:, None] * np.arange(wave_total)[None, :] % lon_size
    angle = np.float32(2.0 * math.pi / lon_size) * phase.astype(np.float32)
    table = np.stack([np.cos(angle), -np.sin(angle)], axis=1) / np.float32(math.sqrt(lon_size))
    return table.astype(jnp.bfloat16)


def merid_table(lat_size, wave_total):
    wave_index = np.arange(wave_total) - wave_total // 2
    phase = np.arange(lat_size)[:, None] * wave_index[None, :] % lat_size
    angle = np.float32(2.0 * math.pi / lat_size) * phase.astype(np.float32)
    table = np.stack([np.cos(angle), np.sin(angle)], axis=1) / np.float32(math.sqrt(lat_size))
    return table.astype(jnp.bfloat16)


def swap_core(block, level_size):
    return lax.ppermute(block, "level", [(i, i ^ 1) for i in range(level_size)])


def from_chip(block, level_size, distance):
    return lax.ppermute(
        block, "level", [((i + 2 * distance) % level_size, i) for i in range(level_size)]
    )


def cross_pair(own_spec, other_spec):
    own = own_spec.astype(jnp.float32)
    other = other_spec.astype(jnp.float32)
    scale = 1.0 / own.shape[1]
    co_spec = (own[0] * other[0] + own[1] * other[1]).sum(axis=0) * scale
    quad_spec = (own[1] * other[0] - own[0] * other[1]).sum(axis=0) * scale
    return jnp.stack([co_spec, quad_spec])


def by_collectives(fc_long, fc_short):
    lat_local, lev_local, sample_count, var_count, lon_size = fc_long.shape
    space_size = lax.axis_size("space")
    level_size = lax.axis_size("level")
    wave_local = MK // space_size
    lat_total = lat_local * space_size
    zonal_tab = zonal_table(lon_size, MK).reshape(lon_size, 2, space_size, wave_local)
    zonal_tab = zonal_tab.transpose(0, 2, 1, 3)
    merid_tab = merid_table(lat_total, NL)
    core = lax.axis_index("level") % 2
    chip = lax.axis_index("level") // 2

    per_var = []
    for var in range(var_count):
        diff = (
            fc_long[:, 0, :, var].astype(jnp.float32) - fc_short[:, 0, :, var].astype(jnp.float32)
        ).astype(jnp.bfloat16)
        coeff = jnp.einsum(
            "ysx,xpuk->pysuk", diff, zonal_tab, preferred_element_type=jnp.float32
        ).astype(jnp.bfloat16)
        coeff = coeff.reshape(space_size * lat_local, sample_count * 2 * wave_local)
        columns = lax.all_to_all(coeff, "space", split_axis=0, concat_axis=0, tiled=True)
        products = jnp.einsum(
            "yn,ytl->ntl", columns, merid_tab, preferred_element_type=jnp.float32
        ).reshape(sample_count, 2, wave_local, 2, NL)
        real_part = products[:, 0, :, 0] + products[:, 1, :, 1]
        imag_part = products[:, 1, :, 0] - products[:, 0, :, 1]
        spectra = jnp.stack([real_part, imag_part]).astype(jnp.bfloat16)
        pairs = []
        for distance in range(level_size // 2):
            mine = spectra if distance == 0 else from_chip(spectra, level_size, distance)
            pairs.append((mine, swap_core(mine, level_size)))
        blocks = []
        for mine, mate in pairs:
            one = cross_pair(spectra, mine)
            two = cross_pair(spectra, mate)
            blocks.append(jnp.where(core == 0, one, two))
            blocks.append(jnp.where(core == 0, two, one))
        per_var.append(jnp.stack(blocks, axis=1))
    assembled = jnp.stack(per_var, axis=1)
    assembled = jnp.roll(assembled, 2 * chip, axis=2)
    return assembled[:, :, None]


LANES = 128
MESH = pl.DeviceIdType.MESH
BLOCKS = ((7, 3, 1), (0, 2, 0), (2, 2, 0), (4, 2, 0), (6, 1, 0))
HALF = len(BLOCKS)
TILES = 10
SAMPLES = 8


def kernel(
    space_size, lat, wave, long_hbm, short_hbm, tab_hbm, merid_hbm, merid_half_hbm, out_ref,
    long_in, short_in, tab, merid, merid_half, diff, zbuf,
    send, recv, spec, send_half, recv_half, spec_half, acc,
    in_sem, tab_sem, merid_sem,
    a2a_send, a2a_recv, own_sem, mate_send, mate_recv, far_send, far_recv, fwd_send, fwd_recv,
):
    me = lax.axis_index("space")
    level = lax.axis_index("level")
    mate = level + 1 - 2 * lax.rem(level, 2)
    far = lax.rem(level + 2, 4)
    far_mate = lax.rem(mate + 2, 4)
    rows = 2 * lat
    half = NL
    pairs = space_size // 2
    padded = recv_half.shape[0] // space_size
    own_half = pl.ds(pl.multiple_of(me * padded, 16), padded)
    own_rows = pl.ds(pl.multiple_of(me * rows, 16), rows)

    def load(var):
        return (
            pltpu.make_async_copy(long_hbm.at[:, var], long_in.at[var], in_sem.at[0, var]),
            pltpu.make_async_copy(short_hbm.at[:, var], short_in.at[var], in_sem.at[1, var]),
        )

    load_tab = pltpu.make_async_copy(tab_hbm, tab, tab_sem)
    load_merid = pltpu.make_async_copy(merid_hbm, merid, merid_sem.at[0])
    load_half = pltpu.make_async_copy(merid_half_hbm, merid_half, merid_sem.at[1])
    for copy in load(2):
        copy.start()
    load_tab.start()

    barrier = pltpu.get_barrier_semaphore()
    for d in range(1, space_size):
        peer = lax.rem(me + d, space_size)
        pl.semaphore_signal(barrier, inc=1, device_id={"space": peer}, device_id_type=MESH)
    for peer in (mate, far):
        pl.semaphore_signal(barrier, inc=1, device_id={"level": peer}, device_id_type=MESH)

    def columns(block):
        first, count, _ = BLOCKS[block]
        return pl.ds(first * LANES, count * LANES)

    def to_peer(block, d):
        peer = lax.rem(me + d, space_size)
        if block == HALF:
            source, target = send_half.at[peer], recv_half.at[own_half]
        else:
            cols = columns(block)
            source, target = send.at[peer, :, cols], recv.at[own_rows, cols]
        return pltpu.make_async_remote_copy(
            src_ref=source,
            dst_ref=target,
            send_sem=a2a_send.at[block, d],
            recv_sem=a2a_recv.at[block, d],
            device_id={"space": peer},
            device_id_type=MESH,
        )

    def to_self(block):
        if block == HALF:
            return pltpu.make_async_copy(
                send_half.at[me], recv_half.at[own_half], own_sem.at[block]
            )
        cols = columns(block)
        return pltpu.make_async_copy(
            send.at[me, :, cols], recv.at[own_rows, cols], own_sem.at[block]
        )

    def to_level(block, peer, source, slot, send_sem, recv_sem):
        if block == HALF:
            first, second = spec_half.at[source], spec_half.at[slot]
        else:
            cols = columns(block)
            first, second = spec.at[source, :, cols], spec.at[slot, :, cols]
        return pltpu.make_async_remote_copy(
            src_ref=first,
            dst_ref=second,
            send_sem=send_sem.at[block],
            recv_sem=recv_sem.at[block],
            device_id={"level": peer},
            device_id_type=MESH,
        )

    def to_mate(block):
        return to_level(block, mate, 0, 1, mate_send, mate_recv)

    def to_far(block):
        return to_level(block, far, 0, 2, far_send, far_recv)

    def forward(block):
        return to_level(block, mate, 2, 3, fwd_send, fwd_recv)

    def difference(var):
        def part(r, carry):
            lats = pl.ds(r * 8, 8)
            delta = long_in[var, lats].astype(jnp.float32) - short_in[var, lats].astype(jnp.float32)
            delta = delta.reshape(8 * SAMPLES, delta.shape[-1]).astype(jnp.bfloat16)
            diff[var, pl.ds(pl.multiple_of(r * 8 * SAMPLES, 8 * SAMPLES), 8 * SAMPLES), :] = delta
            return carry

        lax.fori_loop(0, lat // 8, part, 0)

    def zonal(var, slot, pair):
        def part(r, carry):
            some = pl.ds(pl.multiple_of(r * rows, 16), rows)
            z = jnp.dot(diff[var, some, :], tab[pair], preferred_element_type=jnp.float32)
            zbuf[slot, 0, some, :] = z[:, :LANES]
            zbuf[slot, 1, some, :] = z[:, LANES:]
            return carry

        lax.fori_loop(0, SAMPLES // 2, part, 0)

    def merged(slot0, s0, slot1, s1, j):
        lane = lax.broadcasted_iota(jnp.int32, (lat, LANES), 1)
        one = zbuf[slot0, j, pl.ds(s0, lat, stride=SAMPLES), :]
        two = zbuf[slot1, j, pl.ds(s1, lat, stride=SAMPLES), :]
        real = jnp.where(lane < wave, one, pltpu.roll(two, wave, 1))
        imag = jnp.where(lane < wave, pltpu.roll(one, LANES - wave, 1), two)
        return jnp.concatenate([real, imag], axis=0)

    def put(peer, t, tile, spread, part):
        lane = lax.broadcasted_iota(jnp.int32, (rows, LANES), 1)
        extra = pltpu.roll(spread, 2 * wave - 16 * part, 1)
        tile = jnp.where(lane < 2 * wave, tile, extra)
        send[peer, :, t * LANES : (t + 1) * LANES] = tile.astype(jnp.bfloat16)

    def start_peer(block, peer):
        d = lax.rem(peer - me + space_size, space_size)

        @pl.when(peer != me)
        def _():
            to_peer(block, d).start()

    def single_tiles(i, carry):
        pair = lax.rem(me // 2 + 1 + i, pairs)
        zonal(2, 0, pair)
        lane = lax.broadcasted_iota(jnp.int32, (lat, LANES), 1)
        for j in range(2):
            peer = 2 * pair + j
            spread = merged(0, 3, 0, 7, j)
            for t in range(3):
                put(peer, 7 + t, merged(0, t, 0, t + 4, j), spread, t)
            start_peer(0, peer)
            rest = jnp.where(
                lane < 64,
                pltpu.roll(spread[:lat], LANES - 48, 1),
                pltpu.roll(spread[lat:], 64 - 48, 1),
            )
            rest = jnp.concatenate([rest, jnp.zeros((padded - lat, LANES), jnp.float32)], axis=0)
            send_half[peer] = rest.astype(jnp.bfloat16)
        return carry

    def pair_tiles(i, carry):
        pair = lax.rem(me // 2 + 1 + i, pairs)
        zonal(0, 0, pair)
        zonal(1, 1, pair)
        for j in range(2):
            peer = 2 * pair + j
            spread = merged(0, 7, 1, 7, j)
            for t in range(7):
                put(peer, t, merged(0, t, 1, t, j), spread, t)
            start_peer(1, peer)
        return carry

    for copy in load(2):
        copy.wait()
    load_tab.wait()
    for copy in load(0) + load(1):
        copy.start()
    load_merid.start()
    load_half.start()
    difference(2)
    pl.semaphore_wait(barrier, space_size + 1)
    lax.fori_loop(0, pairs, single_tiles, 0)
    for var in (0, 1):
        for copy in load(var):
            copy.wait()
        difference(var)
    lax.fori_loop(0, pairs, pair_tiles, 0)
    for block in range(2, HALF + 1):
        for d in range(1, space_size):
            to_peer(block, lax.rem(d + 1, space_size - 1) + 1).start()
    for block in range(HALF + 1):
        to_self(block).start()
    load_merid.wait()
    load_half.wait()

    def arrive(block):
        for d in range(1, space_size):
            to_peer(block, d).wait_recv()
        to_self(block).wait()

    def share(block):
        to_far(block).start()
        to_mate(block).start()

    def meridional(block):
        first, count, _ = BLOCKS[block]
        cols = slice(first * LANES, (first + count) * LANES)
        arrive(block)

        def part(r, carry):
            r_rows = pl.ds(pl.multiple_of(r * 256, 256), 256)
            total = jnp.dot(merid[r_rows, :], recv[:, cols], preferred_element_type=jnp.float32)
            spec[0, r_rows, cols] = total.astype(jnp.bfloat16)
            return carry

        lax.fori_loop(0, 2 * half // 256, part, 0)
        share(block)

    def meridional_half():
        arrive(HALF)
        lane = lax.broadcasted_iota(jnp.int32, (half, LANES), 1)
        total = jnp.dot(merid_half[...], recv_half[...], preferred_element_type=jnp.float32)
        turned = pltpu.roll(total[half:], 64, 1)
        both = total[:half] + jnp.where(lane < 64, turned, -turned)
        spec_half[0] = both.astype(jnp.bfloat16)
        share(HALF)

    def cross_half(slot):
        step_rows = 64

        def part(r, carry):
            some = pl.ds(pl.multiple_of(r * step_rows, step_rows), step_rows)
            lane = lax.broadcasted_iota(jnp.int32, (step_rows, LANES), 1)
            here = (lane >= 48) & (lane < 48 + 64)
            a = spec_half[0, some, :].astype(jnp.float32)
            b = spec_half[slot, some, :].astype(jnp.float32)
            same = a * b
            mixed = a * pltpu.roll(b, 64, 1)
            co = same + pltpu.roll(same, 64, 1)
            quad = pltpu.roll(mixed, 64, 1) - mixed
            acc[1, 0, slot, some, :] += jnp.where(here, pltpu.roll(co, 48, 1), 0.0)
            acc[1, 1, slot, some, :] += jnp.where(here, pltpu.roll(quad, 48, 1), 0.0)
            return carry

        lax.fori_loop(0, half // step_rows, part, 0)

    def cross(block):
        first, count, group = BLOCKS[block]
        fresh = block == [g for _, _, g in BLOCKS].index(group)
        step_rows = 32

        def part(r, carry):
            base = pl.multiple_of(r * step_rows, step_rows)
            re_rows = pl.ds(base, step_rows)
            im_rows = pl.ds(pl.multiple_of(half + r * step_rows, step_rows), step_rows)
            lane = lax.broadcasted_iota(jnp.int32, (step_rows, LANES), 1)
            for slot in range(4):
                co_sum = quad_sum = None
                for i in range(count):
                    t = first + i
                    cols = slice(t * LANES, (t + 1) * LANES)
                    a_re = spec[0, re_rows, cols].astype(jnp.float32)
                    a_im = spec[0, im_rows, cols].astype(jnp.float32)
                    b_re = spec[slot, re_rows, cols].astype(jnp.float32)
                    b_im = spec[slot, im_rows, cols].astype(jnp.float32)
                    co = a_re * b_re + a_im * b_im
                    quad = a_im * b_re - a_re * b_im
                    low = 16 * (t - 7 * group)
                    here = (lane >= low) & (lane < low + 16)
                    co = co + jnp.where(here, pltpu.roll(co, low + 16, 1), 0.0)
                    quad = quad + jnp.where(here, pltpu.roll(quad, low + 16, 1), 0.0)
                    co_sum = co if co_sum is None else co_sum + co
                    quad_sum = quad if quad_sum is None else quad_sum + quad
                if fresh:
                    acc[group, 0, slot, re_rows, :] = co_sum
                    acc[group, 1, slot, re_rows, :] = quad_sum
                else:
                    acc[group, 0, slot, re_rows, :] += co_sum
                    acc[group, 1, slot, re_rows, :] += quad_sum
            return carry

        lax.fori_loop(0, half // step_rows, part, 0)

    scale = 1.0 / SAMPLES

    def write(slot, b):
        for c in range(2):
            pair = acc[0, c, slot].T * scale
            single = acc[1, c, slot].T * scale
            out_ref[c, 0, b] = pair[:wave]
            out_ref[c, 1, b] = pair[wave : 2 * wave]
            out_ref[c, 2, b] = single[:wave] + single[wave : 2 * wave]

    def relay(block):
        to_far(block).wait_recv()
        forward(block).start()

    def finish(block):
        to_mate(block).wait_recv()
        forward(block).wait_recv()
        cross(block)

    for block in range(HALF):
        meridional(block)
        if block >= 1:
            relay(block - 1)
        if block >= 2:
            finish(block - 2)
    finish(HALF - 2)
    relay(HALF - 1)
    meridional_half()
    finish(HALF - 1)
    cross_half(0)
    write(0, level)
    to_mate(HALF).wait_recv()
    cross_half(1)
    relay(HALF)
    write(1, mate)
    cross_half(2)
    write(2, far)
    forward(HALF).wait_recv()
    cross_half(3)
    write(3, far_mate)

    for block in range(HALF + 1):
        for d in range(1, space_size):
            to_peer(block, d).wait_send()
        to_mate(block).wait_send()
        to_far(block).wait_send()
        forward(block).wait_send()


def by_kernel(fc_long, fc_short):
    lat, lev_local, sample_count, var_count, lon_size = fc_long.shape
    space_size = lax.axis_size("space")
    wave = MK // space_size
    pairs = space_size // 2
    rows = 2 * lat
    bf16 = jnp.bfloat16
    table = zonal_table(lon_size, MK).reshape(lon_size, 2, pairs, 2, wave).transpose(2, 0, 3, 1, 4)
    padded = np.zeros((pairs, lon_size, 2, LANES), jnp.bfloat16)
    padded[..., : 2 * wave] = table.reshape(pairs, lon_size, 2, 2 * wave)
    padded = padded.reshape(pairs, lon_size, 2 * LANES)
    merid = merid_table(lat * space_size, NL).reshape(space_size, lat, 2, NL)
    cos, sin = merid[:, :, 0], merid[:, :, 1]
    stacked = np.stack([np.stack([cos, sin], axis=1), np.stack([-sin, cos], axis=1)])
    stacked = stacked.transpose(0, 4, 1, 2, 3).reshape(2 * NL, space_size * rows)
    row_pad = -(-lat // 16) * 16
    halves = np.zeros((2, NL, space_size, row_pad), bf16)
    halves[..., :lat] = np.stack([cos, sin]).transpose(0, 3, 1, 2)
    halves = halves.reshape(2 * NL, space_size * row_pad)
    blocks = HALF + 1
    sems = pltpu.SemaphoreType.DMA
    out = pl.pallas_call(
        functools.partial(kernel, space_size, lat, wave),
        out_shape=jax.ShapeDtypeStruct((2, var_count, 4, wave, NL), jnp.float32),
        in_specs=[pl.BlockSpec(memory_space=pl.ANY)] * 5,
        out_specs=pl.BlockSpec(memory_space=pltpu.VMEM),
        scratch_shapes=[
            pltpu.VMEM((var_count, lat, sample_count, lon_size), bf16),
            pltpu.VMEM((var_count, lat, sample_count, lon_size), bf16),
            pltpu.VMEM(padded.shape, bf16),
            pltpu.VMEM(stacked.shape, bf16),
            pltpu.VMEM(halves.shape, bf16),
            pltpu.VMEM((var_count, lat * sample_count, lon_size), bf16),
            pltpu.VMEM((2, 2, lat * sample_count, LANES), jnp.float32),
            pltpu.VMEM((space_size, rows, TILES * LANES), bf16),
            pltpu.VMEM((space_size * rows, TILES * LANES), bf16),
            pltpu.VMEM((4, 2 * NL, TILES * LANES), bf16),
            pltpu.VMEM((space_size, row_pad, LANES), bf16),
            pltpu.VMEM((space_size * row_pad, LANES), bf16),
            pltpu.VMEM((4, NL, LANES), bf16),
            pltpu.VMEM((2, 2, 4, NL, LANES), jnp.float32),
            sems((2, var_count)),
            sems,
            sems((2,)),
            sems((blocks, space_size)),
            sems((blocks, space_size)),
        ]
        + [sems((blocks,))] * 7,
        compiler_params=pltpu.CompilerParams(
            collective_id=0, has_side_effects=True, vmem_limit_bytes=58 * 1024 * 1024
        ),
    )(
        fc_long[:, 0].transpose(0, 2, 1, 3),
        fc_short[:, 0].transpose(0, 2, 1, 3),
        jnp.asarray(padded),
        jnp.asarray(stacked),
        jnp.asarray(halves),
    )
    return out[:, :, None]


def on_device(fc_long, fc_short):
    lat, lev_local, sample_count, var_count, lon_size = fc_long.shape
    space_size = lax.axis_size("space")
    fits = (
        lat % 8 == 0
        and 2 * (MK // space_size) == LANES - 16
        and (lev_local, sample_count, var_count) == (1, SAMPLES, 3)
        and space_size % 2 == 0
        and lax.axis_size("level") == 4
        and 2 * NL % 256 == 0
    )
    return by_kernel(fc_long, fc_short) if fits else by_collectives(fc_long, fc_short)


def solution(mesh):
    placed = (P("space", "level", None, None, None), P("space", "level", None, None, None))
    return jax.shard_map(
        on_device,
        mesh=mesh,
        in_specs=placed,
        out_specs=P(None, None, "level", None, "space", None),
        check_vma=False,
    )
```

```python
import functools
import math

import jax
import jax.numpy as jnp
import numpy as np
from jax import lax
from jax.experimental import pallas as pl
from jax.experimental.pallas import tpu as pltpu
from jax.sharding import PartitionSpec as P

MK = 448
NL = 384


def zonal_table(lon_size, wave_total):
    phase = np.arange(lon_size)[:, None] * np.arange(wave_total)[None, :] % lon_size
    angle = np.float32(2.0 * math.pi / lon_size) * phase.astype(np.float32)
    table = np.stack([np.cos(angle), -np.sin(angle)], axis=1) / np.float32(math.sqrt(lon_size))
    return table.astype(jnp.bfloat16)


def merid_table(lat_size, wave_total):
    wave_index = np.arange(wave_total) - wave_total // 2
    phase = np.arange(lat_size)[:, None] * wave_index[None, :] % lat_size
    angle = np.float32(2.0 * math.pi / lat_size) * phase.astype(np.float32)
    table = np.stack([np.cos(angle), np.sin(angle)], axis=1) / np.float32(math.sqrt(lat_size))
    return table.astype(jnp.bfloat16)


def swap_core(block, level_size):
    return lax.ppermute(block, "level", [(i, i ^ 1) for i in range(level_size)])


def from_chip(block, level_size, distance):
    return lax.ppermute(
        block, "level", [((i + 2 * distance) % level_size, i) for i in range(level_size)]
    )


def cross_pair(own_spec, other_spec):
    own = own_spec.astype(jnp.float32)
    other = other_spec.astype(jnp.float32)
    scale = 1.0 / own.shape[1]
    co_spec = (own[0] * other[0] + own[1] * other[1]).sum(axis=0) * scale
    quad_spec = (own[1] * other[0] - own[0] * other[1]).sum(axis=0) * scale
    return jnp.stack([co_spec, quad_spec])


def by_collectives(fc_long, fc_short):
    lat_local, lev_local, sample_count, var_count, lon_size = fc_long.shape
    space_size = lax.axis_size("space")
    level_size = lax.axis_size("level")
    wave_local = MK // space_size
    lat_total = lat_local * space_size
    zonal_tab = zonal_table(lon_size, MK).reshape(lon_size, 2, space_size, wave_local)
    zonal_tab = zonal_tab.transpose(0, 2, 1, 3)
    merid_tab = merid_table(lat_total, NL)
    core = lax.axis_index("level") % 2
    chip = lax.axis_index("level") // 2

    per_var = []
    for var in range(var_count):
        diff = (
            fc_long[:, 0, :, var].astype(jnp.float32) - fc_short[:, 0, :, var].astype(jnp.float32)
        ).astype(jnp.bfloat16)
        coeff = jnp.einsum(
            "ysx,xpuk->pysuk", diff, zonal_tab, preferred_element_type=jnp.float32
        ).astype(jnp.bfloat16)
        coeff = coeff.reshape(space_size * lat_local, sample_count * 2 * wave_local)
        columns = lax.all_to_all(coeff, "space", split_axis=0, concat_axis=0, tiled=True)
        products = jnp.einsum(
            "yn,ytl->ntl", columns, merid_tab, preferred_element_type=jnp.float32
        ).reshape(sample_count, 2, wave_local, 2, NL)
        real_part = products[:, 0, :, 0] + products[:, 1, :, 1]
        imag_part = products[:, 1, :, 0] - products[:, 0, :, 1]
        spectra = jnp.stack([real_part, imag_part]).astype(jnp.bfloat16)
        pairs = []
        for distance in range(level_size // 2):
            mine = spectra if distance == 0 else from_chip(spectra, level_size, distance)
            pairs.append((mine, swap_core(mine, level_size)))
        blocks = []
        for mine, mate in pairs:
            one = cross_pair(spectra, mine)
            two = cross_pair(spectra, mate)
            blocks.append(jnp.where(core == 0, one, two))
            blocks.append(jnp.where(core == 0, two, one))
        per_var.append(jnp.stack(blocks, axis=1))
    assembled = jnp.stack(per_var, axis=1)
    assembled = jnp.roll(assembled, 2 * chip, axis=2)
    return assembled[:, :, None]


LANES = 128
MESH = pl.DeviceIdType.MESH
BLOCKS = ((7, 3, 1), (0, 2, 0), (2, 2, 0), (4, 2, 0), (6, 1, 0))
HALF = len(BLOCKS)
TILES = 10
SAMPLES = 8
IN_FLIGHT = 3


def kernel(
    space_size, lat, wave, long_hbm, short_hbm, tab_hbm, merid_hbm, merid_half_hbm, out_ref,
    long_in, short_in, tab, merid, merid_half, diff, zbuf,
    send, recv, spec, send_half, recv_half, spec_half, acc,
    in_sem, tab_sem, merid_sem,
    a2a_send, a2a_recv, own_sem, mate_send, mate_recv, far_send, far_recv, fwd_send, fwd_recv,
):
    me = lax.axis_index("space")
    level = lax.axis_index("level")
    mate = level + 1 - 2 * lax.rem(level, 2)
    far = lax.rem(level + 2, 4)
    far_mate = lax.rem(mate + 2, 4)
    rows = 2 * lat
    half = NL
    pairs = space_size // 2
    padded = recv_half.shape[0] // space_size
    own_half = pl.ds(pl.multiple_of(me * padded, 16), padded)
    own_rows = pl.ds(pl.multiple_of(me * rows, 16), rows)

    def load(var):
        return (
            pltpu.make_async_copy(long_hbm.at[:, var], long_in.at[var], in_sem.at[0, var]),
            pltpu.make_async_copy(short_hbm.at[:, var], short_in.at[var], in_sem.at[1, var]),
        )

    load_tab = pltpu.make_async_copy(tab_hbm, tab, tab_sem)
    load_merid = pltpu.make_async_copy(merid_hbm, merid, merid_sem.at[0])
    load_half = pltpu.make_async_copy(merid_half_hbm, merid_half, merid_sem.at[1])
    for copy in load(2):
        copy.start()
    load_tab.start()

    barrier = pltpu.get_barrier_semaphore()
    for d in range(1, space_size):
        peer = lax.rem(me + d, space_size)
        pl.semaphore_signal(barrier, inc=1, device_id={"space": peer}, device_id_type=MESH)
    for peer in (mate, far):
        pl.semaphore_signal(barrier, inc=1, device_id={"level": peer}, device_id_type=MESH)

    def columns(block):
        first, count, _ = BLOCKS[block]
        return pl.ds(first * LANES, count * LANES)

    def to_peer(block, d):
        peer = lax.rem(me + d, space_size)
        if block == HALF:
            source, target = send_half.at[peer], recv_half.at[own_half]
        else:
            cols = columns(block)
            source, target = send.at[peer, :, cols], recv.at[own_rows, cols]
        return pltpu.make_async_remote_copy(
            src_ref=source,
            dst_ref=target,
            send_sem=a2a_send.at[block, d],
            recv_sem=a2a_recv.at[block, d],
            device_id={"space": peer},
            device_id_type=MESH,
        )

    def to_self(block):
        if block == HALF:
            return pltpu.make_async_copy(
                send_half.at[me], recv_half.at[own_half], own_sem.at[block]
            )
        cols = columns(block)
        return pltpu.make_async_copy(
            send.at[me, :, cols], recv.at[own_rows, cols], own_sem.at[block]
        )

    def to_level(block, peer, source, slot, send_sem, recv_sem):
        if block == HALF:
            first, second = spec_half.at[source], spec_half.at[slot]
        else:
            cols = columns(block)
            first, second = spec.at[source, :, cols], spec.at[slot, :, cols]
        return pltpu.make_async_remote_copy(
            src_ref=first,
            dst_ref=second,
            send_sem=send_sem.at[block],
            recv_sem=recv_sem.at[block],
            device_id={"level": peer},
            device_id_type=MESH,
        )

    def to_mate(block):
        return to_level(block, mate, 0, 1, mate_send, mate_recv)

    def to_far(block):
        return to_level(block, far, 0, 2, far_send, far_recv)

    def forward(block):
        return to_level(block, mate, 2, 3, fwd_send, fwd_recv)

    def difference(var):
        def part(r, carry):
            lats = pl.ds(r * 8, 8)
            delta = long_in[var, lats].astype(jnp.float32) - short_in[var, lats].astype(jnp.float32)
            delta = delta.reshape(8 * SAMPLES, delta.shape[-1]).astype(jnp.bfloat16)
            diff[var, pl.ds(pl.multiple_of(r * 8 * SAMPLES, 8 * SAMPLES), 8 * SAMPLES), :] = delta
            return carry

        lax.fori_loop(0, lat // 8, part, 0)

    def zonal(var, slot, pair):
        def part(r, carry):
            some = pl.ds(pl.multiple_of(r * rows, 16), rows)
            z = jnp.dot(diff[var, some, :], tab[pair], preferred_element_type=jnp.float32)
            zbuf[slot, 0, some, :] = z[:, :LANES]
            zbuf[slot, 1, some, :] = z[:, LANES:]
            return carry

        lax.fori_loop(0, SAMPLES // 2, part, 0)

    def merged(slot0, s0, slot1, s1, j):
        lane = lax.broadcasted_iota(jnp.int32, (lat, LANES), 1)
        one = zbuf[slot0, j, pl.ds(s0, lat, stride=SAMPLES), :]
        two = zbuf[slot1, j, pl.ds(s1, lat, stride=SAMPLES), :]
        real = jnp.where(lane < wave, one, pltpu.roll(two, wave, 1))
        imag = jnp.where(lane < wave, pltpu.roll(one, LANES - wave, 1), two)
        return jnp.concatenate([real, imag], axis=0)

    def put(peer, t, tile, spread, part):
        lane = lax.broadcasted_iota(jnp.int32, (rows, LANES), 1)
        extra = pltpu.roll(spread, 2 * wave - 16 * part, 1)
        tile = jnp.where(lane < 2 * wave, tile, extra)
        send[peer, :, t * LANES : (t + 1) * LANES] = tile.astype(jnp.bfloat16)

    def start_peer(block, peer):
        d = lax.rem(peer - me + space_size, space_size)

        @pl.when(peer != me)
        def _():
            to_peer(block, d).start()

    def pair_at(i):
        place = me // 2
        middle = pairs // 2
        upper = place // middle
        depth = place + upper * (pairs - 1 - 2 * place)
        order = lax.rem(i + middle * lax.rem(depth + 1, 2), pairs)
        return order + upper * (pairs - 1 - 2 * order)

    def start_block(block):
        def one_pair(i, carry):
            pair = pair_at(i)
            for j in range(2):
                start_peer(block, 2 * pair + j)
            return carry

        lax.fori_loop(0, pairs, one_pair, 0)

    def single_tiles(i, carry):
        pair = pair_at(i)
        zonal(2, 0, pair)
        lane = lax.broadcasted_iota(jnp.int32, (lat, LANES), 1)
        for j in range(2):
            peer = 2 * pair + j
            spread = merged(0, 3, 0, 7, j)
            for t in range(3):
                put(peer, 7 + t, merged(0, t, 0, t + 4, j), spread, t)
            start_peer(0, peer)
            rest = jnp.where(
                lane < 64,
                pltpu.roll(spread[:lat], LANES - 48, 1),
                pltpu.roll(spread[lat:], 64 - 48, 1),
            )
            rest = jnp.concatenate([rest, jnp.zeros((padded - lat, LANES), jnp.float32)], axis=0)
            send_half[peer] = rest.astype(jnp.bfloat16)
        return carry

    def pair_tiles(i, carry):
        pair = pair_at(i)
        zonal(0, 0, pair)
        zonal(1, 1, pair)
        for j in range(2):
            peer = 2 * pair + j
            spread = merged(0, 7, 1, 7, j)
            for t in range(7):
                put(peer, t, merged(0, t, 1, t, j), spread, t)
            start_peer(1, peer)
        return carry

    for copy in load(2):
        copy.wait()
    load_tab.wait()
    for copy in load(0) + load(1):
        copy.start()
    load_merid.start()
    load_half.start()
    difference(2)
    pl.semaphore_wait(barrier, space_size + 1)
    lax.fori_loop(0, pairs, single_tiles, 0)
    for var in (0, 1):
        for copy in load(var):
            copy.wait()
        difference(var)
    lax.fori_loop(0, pairs, pair_tiles, 0)
    for block in range(2, IN_FLIGHT):
        start_block(block)
    for block in range(HALF + 1):
        to_self(block).start()
    load_merid.wait()
    load_half.wait()

    def arrive(block):
        for d in range(1, space_size):
            to_peer(block, d).wait_recv()
        if block + IN_FLIGHT <= HALF:
            start_block(block + IN_FLIGHT)
        to_self(block).wait()

    def share(block):
        to_far(block).start()
        to_mate(block).start()

    def meridional(block):
        first, count, _ = BLOCKS[block]
        cols = slice(first * LANES, (first + count) * LANES)
        arrive(block)

        def part(r, carry):
            r_rows = pl.ds(pl.multiple_of(r * 256, 256), 256)
            total = jnp.dot(merid[r_rows, :], recv[:, cols], preferred_element_type=jnp.float32)
            spec[0, r_rows, cols] = total.astype(jnp.bfloat16)
            return carry

        lax.fori_loop(0, 2 * half // 256, part, 0)
        share(block)

    def meridional_half():
        arrive(HALF)
        lane = lax.broadcasted_iota(jnp.int32, (half, LANES), 1)
        total = jnp.dot(merid_half[...], recv_half[...], preferred_element_type=jnp.float32)
        turned = pltpu.roll(total[half:], 64, 1)
        both = total[:half] + jnp.where(lane < 64, turned, -turned)
        spec_half[0] = both.astype(jnp.bfloat16)
        share(HALF)

    def cross_half(slot):
        step_rows = 64

        def part(r, carry):
            some = pl.ds(pl.multiple_of(r * step_rows, step_rows), step_rows)
            lane = lax.broadcasted_iota(jnp.int32, (step_rows, LANES), 1)
            here = (lane >= 48) & (lane < 48 + 64)
            a = spec_half[0, some, :].astype(jnp.float32)
            b = spec_half[slot, some, :].astype(jnp.float32)
            same = a * b
            mixed = a * pltpu.roll(b, 64, 1)
            co = same + pltpu.roll(same, 64, 1)
            quad = pltpu.roll(mixed, 64, 1) - mixed
            acc[1, 0, slot, some, :] += jnp.where(here, pltpu.roll(co, 48, 1), 0.0)
            acc[1, 1, slot, some, :] += jnp.where(here, pltpu.roll(quad, 48, 1), 0.0)
            return carry

        lax.fori_loop(0, half // step_rows, part, 0)

    def cross(block):
        first, count, group = BLOCKS[block]
        fresh = block == [g for _, _, g in BLOCKS].index(group)
        step_rows = 32

        def part(r, carry):
            base = pl.multiple_of(r * step_rows, step_rows)
            re_rows = pl.ds(base, step_rows)
            im_rows = pl.ds(pl.multiple_of(half + r * step_rows, step_rows), step_rows)
            lane = lax.broadcasted_iota(jnp.int32, (step_rows, LANES), 1)
            for slot in range(4):
                co_sum = quad_sum = None
                for i in range(count):
                    t = first + i
                    cols = slice(t * LANES, (t + 1) * LANES)
                    a_re = spec[0, re_rows, cols].astype(jnp.float32)
                    a_im = spec[0, im_rows, cols].astype(jnp.float32)
                    b_re = spec[slot, re_rows, cols].astype(jnp.float32)
                    b_im = spec[slot, im_rows, cols].astype(jnp.float32)
                    co = a_re * b_re + a_im * b_im
                    quad = a_im * b_re - a_re * b_im
                    low = 16 * (t - 7 * group)
                    here = (lane >= low) & (lane < low + 16)
                    co = co + jnp.where(here, pltpu.roll(co, low + 16, 1), 0.0)
                    quad = quad + jnp.where(here, pltpu.roll(quad, low + 16, 1), 0.0)
                    co_sum = co if co_sum is None else co_sum + co
                    quad_sum = quad if quad_sum is None else quad_sum + quad
                if fresh:
                    acc[group, 0, slot, re_rows, :] = co_sum
                    acc[group, 1, slot, re_rows, :] = quad_sum
                else:
                    acc[group, 0, slot, re_rows, :] += co_sum
                    acc[group, 1, slot, re_rows, :] += quad_sum
            return carry

        lax.fori_loop(0, half // step_rows, part, 0)

    scale = 1.0 / SAMPLES

    def write(slot, b):
        for c in range(2):
            pair = acc[0, c, slot].T * scale
            single = acc[1, c, slot].T * scale
            out_ref[c, 0, b] = pair[:wave]
            out_ref[c, 1, b] = pair[wave : 2 * wave]
            out_ref[c, 2, b] = single[:wave] + single[wave : 2 * wave]

    def relay(block):
        to_far(block).wait_recv()
        forward(block).start()

    def finish(block):
        to_mate(block).wait_recv()
        forward(block).wait_recv()
        cross(block)

    for block in range(HALF):
        meridional(block)
        if block >= 1:
            relay(block - 1)
        if block >= 2:
            finish(block - 2)
    finish(HALF - 2)
    relay(HALF - 1)
    meridional_half()
    finish(HALF - 1)
    cross_half(0)
    write(0, level)
    to_mate(HALF).wait_recv()
    cross_half(1)
    relay(HALF)
    write(1, mate)
    cross_half(2)
    write(2, far)
    forward(HALF).wait_recv()
    cross_half(3)
    write(3, far_mate)

    for block in range(HALF + 1):
        for d in range(1, space_size):
            to_peer(block, d).wait_send()
        to_mate(block).wait_send()
        to_far(block).wait_send()
        forward(block).wait_send()


def by_kernel(fc_long, fc_short):
    lat, lev_local, sample_count, var_count, lon_size = fc_long.shape
    space_size = lax.axis_size("space")
    wave = MK // space_size
    pairs = space_size // 2
    rows = 2 * lat
    bf16 = jnp.bfloat16
    table = zonal_table(lon_size, MK).reshape(lon_size, 2, pairs, 2, wave).transpose(2, 0, 3, 1, 4)
    padded = np.zeros((pairs, lon_size, 2, LANES), jnp.bfloat16)
    padded[..., : 2 * wave] = table.reshape(pairs, lon_size, 2, 2 * wave)
    padded = padded.reshape(pairs, lon_size, 2 * LANES)
    merid = merid_table(lat * space_size, NL).reshape(space_size, lat, 2, NL)
    cos, sin = merid[:, :, 0], merid[:, :, 1]
    stacked = np.stack([np.stack([cos, sin], axis=1), np.stack([-sin, cos], axis=1)])
    stacked = stacked.transpose(0, 4, 1, 2, 3).reshape(2 * NL, space_size * rows)
    row_pad = -(-lat // 16) * 16
    halves = np.zeros((2, NL, space_size, row_pad), bf16)
    halves[..., :lat] = np.stack([cos, sin]).transpose(0, 3, 1, 2)
    halves = halves.reshape(2 * NL, space_size * row_pad)
    blocks = HALF + 1
    sems = pltpu.SemaphoreType.DMA
    out = pl.pallas_call(
        functools.partial(kernel, space_size, lat, wave),
        out_shape=jax.ShapeDtypeStruct((2, var_count, 4, wave, NL), jnp.float32),
        in_specs=[pl.BlockSpec(memory_space=pl.ANY)] * 5,
        out_specs=pl.BlockSpec(memory_space=pltpu.VMEM),
        scratch_shapes=[
            pltpu.VMEM((var_count, lat, sample_count, lon_size), bf16),
            pltpu.VMEM((var_count, lat, sample_count, lon_size), bf16),
            pltpu.VMEM(padded.shape, bf16),
            pltpu.VMEM(stacked.shape, bf16),
            pltpu.VMEM(halves.shape, bf16),
            pltpu.VMEM((var_count, lat * sample_count, lon_size), bf16),
            pltpu.VMEM((2, 2, lat * sample_count, LANES), jnp.float32),
            pltpu.VMEM((space_size, rows, TILES * LANES), bf16),
            pltpu.VMEM((space_size * rows, TILES * LANES), bf16),
            pltpu.VMEM((4, 2 * NL, TILES * LANES), bf16),
            pltpu.VMEM((space_size, row_pad, LANES), bf16),
            pltpu.VMEM((space_size * row_pad, LANES), bf16),
            pltpu.VMEM((4, NL, LANES), bf16),
            pltpu.VMEM((2, 2, 4, NL, LANES), jnp.float32),
            sems((2, var_count)),
            sems,
            sems((2,)),
            sems((blocks, space_size)),
            sems((blocks, space_size)),
        ]
        + [sems((blocks,))] * 7,
        compiler_params=pltpu.CompilerParams(
            collective_id=0, has_side_effects=True, vmem_limit_bytes=58 * 1024 * 1024
        ),
    )(
        fc_long[:, 0].transpose(0, 2, 1, 3),
        fc_short[:, 0].transpose(0, 2, 1, 3),
        jnp.asarray(padded),
        jnp.asarray(stacked),
        jnp.asarray(halves),
    )
    return out[:, :, None]


def on_device(fc_long, fc_short):
    lat, lev_local, sample_count, var_count, lon_size = fc_long.shape
    space_size = lax.axis_size("space")
    fits = (
        lat % 8 == 0
        and 2 * (MK // space_size) == LANES - 16
        and (lev_local, sample_count, var_count) == (1, SAMPLES, 3)
        and space_size % 4 == 0
        and lax.axis_size("level") == 4
        and 2 * NL % 256 == 0
    )
    return by_kernel(fc_long, fc_short) if fits else by_collectives(fc_long, fc_short)


def solution(mesh):
    placed = (P("space", "level", None, None, None), P("space", "level", None, None, None))
    return jax.shard_map(
        on_device,
        mesh=mesh,
        in_specs=placed,
        out_specs=P(None, None, "level", None, "space", None),
        check_vma=False,
    )
```

```python
import functools
import math

import jax
import jax.numpy as jnp
import numpy as np
from jax import lax
from jax.experimental import pallas as pl
from jax.experimental.pallas import tpu as pltpu
from jax.sharding import PartitionSpec as P

MK = 448
NL = 384


def zonal_table(lon_size, wave_total):
    phase = np.arange(lon_size)[:, None] * np.arange(wave_total)[None, :] % lon_size
    angle = np.float32(2.0 * math.pi / lon_size) * phase.astype(np.float32)
    table = np.stack([np.cos(angle), -np.sin(angle)], axis=1) / np.float32(math.sqrt(lon_size))
    return table.astype(jnp.bfloat16)


def merid_table(lat_size, wave_total):
    wave_index = np.arange(wave_total) - wave_total // 2
    phase = np.arange(lat_size)[:, None] * wave_index[None, :] % lat_size
    angle = np.float32(2.0 * math.pi / lat_size) * phase.astype(np.float32)
    table = np.stack([np.cos(angle), np.sin(angle)], axis=1) / np.float32(math.sqrt(lat_size))
    return table.astype(jnp.bfloat16)


def swap_core(block, level_size):
    return lax.ppermute(block, "level", [(i, i ^ 1) for i in range(level_size)])


def from_chip(block, level_size, distance):
    return lax.ppermute(
        block, "level", [((i + 2 * distance) % level_size, i) for i in range(level_size)]
    )


def cross_pair(own_spec, other_spec):
    own = own_spec.astype(jnp.float32)
    other = other_spec.astype(jnp.float32)
    scale = 1.0 / own.shape[1]
    co_spec = (own[0] * other[0] + own[1] * other[1]).sum(axis=0) * scale
    quad_spec = (own[1] * other[0] - own[0] * other[1]).sum(axis=0) * scale
    return jnp.stack([co_spec, quad_spec])


def by_collectives(fc_long, fc_short):
    lat_local, lev_local, sample_count, var_count, lon_size = fc_long.shape
    space_size = lax.axis_size("space")
    level_size = lax.axis_size("level")
    wave_local = MK // space_size
    lat_total = lat_local * space_size
    zonal_tab = zonal_table(lon_size, MK).reshape(lon_size, 2, space_size, wave_local)
    zonal_tab = zonal_tab.transpose(0, 2, 1, 3)
    merid_tab = merid_table(lat_total, NL)
    core = lax.axis_index("level") % 2
    chip = lax.axis_index("level") // 2

    per_var = []
    for var in range(var_count):
        diff = (
            fc_long[:, 0, :, var].astype(jnp.float32) - fc_short[:, 0, :, var].astype(jnp.float32)
        ).astype(jnp.bfloat16)
        coeff = jnp.einsum(
            "ysx,xpuk->pysuk", diff, zonal_tab, preferred_element_type=jnp.float32
        ).astype(jnp.bfloat16)
        coeff = coeff.reshape(space_size * lat_local, sample_count * 2 * wave_local)
        columns = lax.all_to_all(coeff, "space", split_axis=0, concat_axis=0, tiled=True)
        products = jnp.einsum(
            "yn,ytl->ntl", columns, merid_tab, preferred_element_type=jnp.float32
        ).reshape(sample_count, 2, wave_local, 2, NL)
        real_part = products[:, 0, :, 0] + products[:, 1, :, 1]
        imag_part = products[:, 1, :, 0] - products[:, 0, :, 1]
        spectra = jnp.stack([real_part, imag_part]).astype(jnp.bfloat16)
        pairs = []
        for distance in range(level_size // 2):
            mine = spectra if distance == 0 else from_chip(spectra, level_size, distance)
            pairs.append((mine, swap_core(mine, level_size)))
        blocks = []
        for mine, mate in pairs:
            one = cross_pair(spectra, mine)
            two = cross_pair(spectra, mate)
            blocks.append(jnp.where(core == 0, one, two))
            blocks.append(jnp.where(core == 0, two, one))
        per_var.append(jnp.stack(blocks, axis=1))
    assembled = jnp.stack(per_var, axis=1)
    assembled = jnp.roll(assembled, 2 * chip, axis=2)
    return assembled[:, :, None]


LANES = 128
MESH = pl.DeviceIdType.MESH
BLOCKS = ((7, 3, 1), (0, 2, 0), (2, 2, 0), (4, 2, 0), (6, 1, 0))
HALF = len(BLOCKS)
TILES = 10
SAMPLES = 8
IN_FLIGHT = 3


def kernel(
    space_size, lat, wave, long_hbm, short_hbm, tab_hbm, merid_hbm, merid_half_hbm, out_ref,
    long_in, short_in, tab, merid, merid_half, diff, zbuf,
    send, recv, spec, send_half, recv_half, spec_half, acc,
    in_sem, tab_sem, merid_sem,
    a2a_send, a2a_recv, own_sem, mate_send, mate_recv, far_send, far_recv, fwd_send, fwd_recv,
):
    me = lax.axis_index("space")
    level = lax.axis_index("level")
    mate = level + 1 - 2 * lax.rem(level, 2)
    far = lax.rem(level + 2, 4)
    far_mate = lax.rem(mate + 2, 4)
    rows = 2 * lat
    half = NL
    pairs = space_size // 2
    padded = recv_half.shape[0] // space_size
    own_half = pl.ds(pl.multiple_of(me * padded, 16), padded)
    own_rows = pl.ds(pl.multiple_of(me * rows, 16), rows)

    def load(var):
        return (
            pltpu.make_async_copy(long_hbm.at[:, var], long_in.at[var], in_sem.at[0, var]),
            pltpu.make_async_copy(short_hbm.at[:, var], short_in.at[var], in_sem.at[1, var]),
        )

    load_tab = pltpu.make_async_copy(tab_hbm, tab, tab_sem)
    load_merid = pltpu.make_async_copy(merid_hbm, merid, merid_sem.at[0])
    load_half = pltpu.make_async_copy(merid_half_hbm, merid_half, merid_sem.at[1])
    for copy in load(2):
        copy.start()
    load_tab.start()

    barrier = pltpu.get_barrier_semaphore()
    for d in range(1, space_size):
        peer = lax.rem(me + d, space_size)
        pl.semaphore_signal(barrier, inc=1, device_id={"space": peer}, device_id_type=MESH)
    for peer in (mate, far):
        pl.semaphore_signal(barrier, inc=1, device_id={"level": peer}, device_id_type=MESH)

    def columns(block):
        first, count, _ = BLOCKS[block]
        return pl.ds(first * LANES, count * LANES)

    def to_peer(block, d):
        peer = lax.rem(me + d, space_size)
        if block == HALF:
            source, target = send_half.at[peer], recv_half.at[own_half]
        else:
            cols = columns(block)
            source, target = send.at[peer, :, cols], recv.at[own_rows, cols]
        return pltpu.make_async_remote_copy(
            src_ref=source,
            dst_ref=target,
            send_sem=a2a_send.at[block, d],
            recv_sem=a2a_recv.at[block, d],
            device_id={"space": peer},
            device_id_type=MESH,
        )

    def to_self(block):
        if block == HALF:
            return pltpu.make_async_copy(
                send_half.at[me], recv_half.at[own_half], own_sem.at[block]
            )
        cols = columns(block)
        return pltpu.make_async_copy(
            send.at[me, :, cols], recv.at[own_rows, cols], own_sem.at[block]
        )

    def to_level(block, peer, source, slot, send_sem, recv_sem):
        if block == HALF:
            first, second = spec_half.at[source], spec_half.at[slot]
        else:
            cols = columns(block)
            first, second = spec.at[source, :, cols], spec.at[slot, :, cols]
        return pltpu.make_async_remote_copy(
            src_ref=first,
            dst_ref=second,
            send_sem=send_sem.at[block],
            recv_sem=recv_sem.at[block],
            device_id={"level": peer},
            device_id_type=MESH,
        )

    def to_mate(block):
        return to_level(block, mate, 0, 1, mate_send, mate_recv)

    def to_far(block):
        return to_level(block, far, 0, 2, far_send, far_recv)

    def forward(block):
        return to_level(block, mate, 2, 3, fwd_send, fwd_recv)

    def difference(var):
        def part(r, carry):
            lats = pl.ds(r * 8, 8)
            delta = long_in[var, lats].astype(jnp.float32) - short_in[var, lats].astype(jnp.float32)
            delta = delta.reshape(8 * SAMPLES, delta.shape[-1]).astype(jnp.bfloat16)
            diff[var, pl.ds(pl.multiple_of(r * 8 * SAMPLES, 8 * SAMPLES), 8 * SAMPLES), :] = delta
            return carry

        lax.fori_loop(0, lat // 8, part, 0)

    def zonal(var, slot, pair):
        z = jnp.dot(diff[var], tab[pair], preferred_element_type=jnp.float32)
        zbuf[slot, 0] = z[:, :LANES]
        zbuf[slot, 1] = z[:, LANES:]

    def merged(slot0, s0, slot1, s1, j):
        lane = lax.broadcasted_iota(jnp.int32, (lat, LANES), 1)
        one = zbuf[slot0, j, pl.ds(s0, lat, stride=SAMPLES), :]
        two = zbuf[slot1, j, pl.ds(s1, lat, stride=SAMPLES), :]
        real = jnp.where(lane < wave, one, pltpu.roll(two, wave, 1))
        imag = jnp.where(lane < wave, pltpu.roll(one, LANES - wave, 1), two)
        return jnp.concatenate([real, imag], axis=0)

    def put(peer, t, tile, spread, part):
        lane = lax.broadcasted_iota(jnp.int32, (rows, LANES), 1)
        extra = pltpu.roll(spread, 2 * wave - 16 * part, 1)
        tile = jnp.where(lane < 2 * wave, tile, extra)
        send[peer, :, t * LANES : (t + 1) * LANES] = tile.astype(jnp.bfloat16)

    def start_peer(block, peer):
        d = lax.rem(peer - me + space_size, space_size)

        @pl.when(peer != me)
        def _():
            to_peer(block, d).start()

    def pair_at(i):
        place = me // 2
        middle = pairs // 2
        upper = place // middle
        depth = place + upper * (pairs - 1 - 2 * place)
        order = lax.rem(i + middle * lax.rem(depth + 1, 2), pairs)
        return order + upper * (pairs - 1 - 2 * order)

    def start_block(block):
        def one_pair(i, carry):
            pair = pair_at(i)
            for j in range(2):
                start_peer(block, 2 * pair + j)
            return carry

        lax.fori_loop(0, pairs, one_pair, 0)

    def single_tiles(i, carry):
        pair = pair_at(i)
        zonal(2, 0, pair)
        lane = lax.broadcasted_iota(jnp.int32, (lat, LANES), 1)
        for j in range(2):
            peer = 2 * pair + j
            spread = merged(0, 3, 0, 7, j)
            for t in range(3):
                put(peer, 7 + t, merged(0, t, 0, t + 4, j), spread, t)
            start_peer(0, peer)
            rest = jnp.where(
                lane < 64,
                pltpu.roll(spread[:lat], LANES - 48, 1),
                pltpu.roll(spread[lat:], 64 - 48, 1),
            )
            rest = jnp.concatenate([rest, jnp.zeros((padded - lat, LANES), jnp.float32)], axis=0)
            send_half[peer] = rest.astype(jnp.bfloat16)
        return carry

    def pair_tiles(i, carry):
        pair = pair_at(i)
        zonal(0, 0, pair)
        zonal(1, 1, pair)
        for j in range(2):
            peer = 2 * pair + j
            spread = merged(0, 7, 1, 7, j)
            for t in range(7):
                put(peer, t, merged(0, t, 1, t, j), spread, t)
            start_peer(1, peer)
            start_peer(2, peer)
        return carry

    for copy in load(2):
        copy.wait()
    load_tab.wait()
    for copy in load(0) + load(1):
        copy.start()
    load_merid.start()
    load_half.start()
    difference(2)
    pl.semaphore_wait(barrier, space_size + 1)
    lax.fori_loop(0, pairs, single_tiles, 0)
    for var in (0, 1):
        for copy in load(var):
            copy.wait()
        difference(var)

    def arrive(block):
        for d in range(1, space_size):
            to_peer(block, d).wait_recv()
        if block > 0 and block + IN_FLIGHT <= HALF:
            start_block(block + IN_FLIGHT)
        to_self(block).start()
        to_self(block).wait()

    def share(block):
        to_far(block).start()
        to_mate(block).start()

    def meridional(block):
        first, count, _ = BLOCKS[block]
        cols = slice(first * LANES, (first + count) * LANES)
        arrive(block)

        def part(r, carry):
            r_rows = pl.ds(pl.multiple_of(r * 256, 256), 256)
            total = jnp.dot(merid[r_rows, :], recv[:, cols], preferred_element_type=jnp.float32)
            spec[0, r_rows, cols] = total.astype(jnp.bfloat16)
            return carry

        lax.fori_loop(0, 2 * half // 256, part, 0)
        share(block)

    def meridional_half():
        arrive(HALF)
        lane = lax.broadcasted_iota(jnp.int32, (half, LANES), 1)
        total = jnp.dot(merid_half[...], recv_half[...], preferred_element_type=jnp.float32)
        turned = pltpu.roll(total[half:], 64, 1)
        both = total[:half] + jnp.where(lane < 64, turned, -turned)
        spec_half[0] = both.astype(jnp.bfloat16)
        share(HALF)

    def cross_half(slot):
        step_rows = 64

        def part(r, carry):
            some = pl.ds(pl.multiple_of(r * step_rows, step_rows), step_rows)
            lane = lax.broadcasted_iota(jnp.int32, (step_rows, LANES), 1)
            here = (lane >= 48) & (lane < 48 + 64)
            a = spec_half[0, some, :].astype(jnp.float32)
            b = spec_half[slot, some, :].astype(jnp.float32)
            same = a * b
            mixed = a * pltpu.roll(b, 64, 1)
            co = same + pltpu.roll(same, 64, 1)
            quad = pltpu.roll(mixed, 64, 1) - mixed
            acc[1, 0, slot, some, :] += jnp.where(here, pltpu.roll(co, 48, 1), 0.0)
            acc[1, 1, slot, some, :] += jnp.where(here, pltpu.roll(quad, 48, 1), 0.0)
            return carry

        lax.fori_loop(0, half // step_rows, part, 0)

    def cross(block):
        first, count, group = BLOCKS[block]
        fresh = block == [g for _, _, g in BLOCKS].index(group)
        step_rows = 32

        def part(r, carry):
            base = pl.multiple_of(r * step_rows, step_rows)
            re_rows = pl.ds(base, step_rows)
            im_rows = pl.ds(pl.multiple_of(half + r * step_rows, step_rows), step_rows)
            lane = lax.broadcasted_iota(jnp.int32, (step_rows, LANES), 1)
            for slot in range(4):
                co_sum = quad_sum = None
                for i in range(count):
                    t = first + i
                    cols = slice(t * LANES, (t + 1) * LANES)
                    a_re = spec[0, re_rows, cols].astype(jnp.float32)
                    a_im = spec[0, im_rows, cols].astype(jnp.float32)
                    b_re = spec[slot, re_rows, cols].astype(jnp.float32)
                    b_im = spec[slot, im_rows, cols].astype(jnp.float32)
                    co = a_re * b_re + a_im * b_im
                    quad = a_im * b_re - a_re * b_im
                    low = 16 * (t - 7 * group)
                    here = (lane >= low) & (lane < low + 16)
                    co = co + jnp.where(here, pltpu.roll(co, low + 16, 1), 0.0)
                    quad = quad + jnp.where(here, pltpu.roll(quad, low + 16, 1), 0.0)
                    co_sum = co if co_sum is None else co_sum + co
                    quad_sum = quad if quad_sum is None else quad_sum + quad
                if fresh:
                    acc[group, 0, slot, re_rows, :] = co_sum
                    acc[group, 1, slot, re_rows, :] = quad_sum
                else:
                    acc[group, 0, slot, re_rows, :] += co_sum
                    acc[group, 1, slot, re_rows, :] += quad_sum
            return carry

        lax.fori_loop(0, half // step_rows, part, 0)

    scale = 1.0 / SAMPLES

    def write(slot, b):
        for c in range(2):
            pair = acc[0, c, slot].T * scale
            single = acc[1, c, slot].T * scale
            out_ref[c, 0, b] = pair[:wave]
            out_ref[c, 1, b] = pair[wave : 2 * wave]
            out_ref[c, 2, b] = single[:wave] + single[wave : 2 * wave]

    def relay(block):
        to_far(block).wait_recv()
        forward(block).start()

    def finish(block):
        to_mate(block).wait_recv()
        forward(block).wait_recv()
        cross(block)

    lax.fori_loop(0, pairs // 2, pair_tiles, 0)
    load_merid.wait()
    load_half.wait()
    meridional(0)
    lax.fori_loop(pairs // 2, pairs, pair_tiles, 0)
    start_block(IN_FLIGHT)
    for block in range(1, HALF):
        meridional(block)
        relay(block - 1)
        if block >= 2:
            finish(block - 2)
    finish(HALF - 2)
    relay(HALF - 1)
    meridional_half()
    finish(HALF - 1)
    cross_half(0)
    write(0, level)
    to_mate(HALF).wait_recv()
    cross_half(1)
    relay(HALF)
    write(1, mate)
    cross_half(2)
    write(2, far)
    forward(HALF).wait_recv()
    cross_half(3)
    write(3, far_mate)

    for block in range(HALF + 1):
        for d in range(1, space_size):
            to_peer(block, d).wait_send()
        to_mate(block).wait_send()
        to_far(block).wait_send()
        forward(block).wait_send()


def by_kernel(fc_long, fc_short):
    lat, lev_local, sample_count, var_count, lon_size = fc_long.shape
    space_size = lax.axis_size("space")
    wave = MK // space_size
    pairs = space_size // 2
    rows = 2 * lat
    bf16 = jnp.bfloat16
    table = zonal_table(lon_size, MK).reshape(lon_size, 2, pairs, 2, wave).transpose(2, 0, 3, 1, 4)
    padded = np.zeros((pairs, lon_size, 2, LANES), jnp.bfloat16)
    padded[..., : 2 * wave] = table.reshape(pairs, lon_size, 2, 2 * wave)
    padded = padded.reshape(pairs, lon_size, 2 * LANES)
    merid = merid_table(lat * space_size, NL).reshape(space_size, lat, 2, NL)
    cos, sin = merid[:, :, 0], merid[:, :, 1]
    stacked = np.stack([np.stack([cos, sin], axis=1), np.stack([-sin, cos], axis=1)])
    stacked = stacked.transpose(0, 4, 1, 2, 3).reshape(2 * NL, space_size * rows)
    row_pad = -(-lat // 16) * 16
    halves = np.zeros((2, NL, space_size, row_pad), bf16)
    halves[..., :lat] = np.stack([cos, sin]).transpose(0, 3, 1, 2)
    halves = halves.reshape(2 * NL, space_size * row_pad)
    blocks = HALF + 1
    sems = pltpu.SemaphoreType.DMA
    out = pl.pallas_call(
        functools.partial(kernel, space_size, lat, wave),
        out_shape=jax.ShapeDtypeStruct((2, var_count, 4, wave, NL), jnp.float32),
        in_specs=[pl.BlockSpec(memory_space=pl.ANY)] * 5,
        out_specs=pl.BlockSpec(memory_space=pltpu.VMEM),
        scratch_shapes=[
            pltpu.VMEM((var_count, lat, sample_count, lon_size), bf16),
            pltpu.VMEM((var_count, lat, sample_count, lon_size), bf16),
            pltpu.VMEM(padded.shape, bf16),
            pltpu.VMEM(stacked.shape, bf16),
            pltpu.VMEM(halves.shape, bf16),
            pltpu.VMEM((var_count, lat * sample_count, lon_size), bf16),
            pltpu.VMEM((2, 2, lat * sample_count, LANES), jnp.float32),
            pltpu.VMEM((space_size, rows, TILES * LANES), bf16),
            pltpu.VMEM((space_size * rows, TILES * LANES), bf16),
            pltpu.VMEM((4, 2 * NL, TILES * LANES), bf16),
            pltpu.VMEM((space_size, row_pad, LANES), bf16),
            pltpu.VMEM((space_size * row_pad, LANES), bf16),
            pltpu.VMEM((4, NL, LANES), bf16),
            pltpu.VMEM((2, 2, 4, NL, LANES), jnp.float32),
            sems((2, var_count)),
            sems,
            sems((2,)),
            sems((blocks, space_size)),
            sems((blocks, space_size)),
        ]
        + [sems((blocks,))] * 7,
        compiler_params=pltpu.CompilerParams(
            collective_id=0, has_side_effects=True, vmem_limit_bytes=58 * 1024 * 1024
        ),
    )(
        fc_long[:, 0].transpose(0, 2, 1, 3),
        fc_short[:, 0].transpose(0, 2, 1, 3),
        jnp.asarray(padded),
        jnp.asarray(stacked),
        jnp.asarray(halves),
    )
    return out[:, :, None]


def on_device(fc_long, fc_short):
    lat, lev_local, sample_count, var_count, lon_size = fc_long.shape
    space_size = lax.axis_size("space")
    fits = (
        lat % 8 == 0
        and 2 * (MK // space_size) == LANES - 16
        and (lev_local, sample_count, var_count) == (1, SAMPLES, 3)
        and space_size % 4 == 0
        and lax.axis_size("level") == 4
        and 2 * NL % 256 == 0
    )
    return by_kernel(fc_long, fc_short) if fits else by_collectives(fc_long, fc_short)


def solution(mesh):
    placed = (P("space", "level", None, None, None), P("space", "level", None, None, None))
    return jax.shard_map(
        on_device,
        mesh=mesh,
        in_specs=placed,
        out_specs=P(None, None, "level", None, "space", None),
        check_vma=False,
    )
```

```python
import functools
import math

import jax
import jax.numpy as jnp
import numpy as np
from jax import lax
from jax.experimental import pallas as pl
from jax.experimental.pallas import tpu as pltpu
from jax.sharding import PartitionSpec as P

MK = 448
NL = 384


def zonal_table(lon_size, wave_total):
    phase = np.arange(lon_size)[:, None] * np.arange(wave_total)[None, :] % lon_size
    angle = np.float32(2.0 * math.pi / lon_size) * phase.astype(np.float32)
    table = np.stack([np.cos(angle), -np.sin(angle)], axis=1) / np.float32(math.sqrt(lon_size))
    return table.astype(jnp.bfloat16)


def merid_table(lat_size, wave_total):
    wave_index = np.arange(wave_total) - wave_total // 2
    phase = np.arange(lat_size)[:, None] * wave_index[None, :] % lat_size
    angle = np.float32(2.0 * math.pi / lat_size) * phase.astype(np.float32)
    table = np.stack([np.cos(angle), np.sin(angle)], axis=1) / np.float32(math.sqrt(lat_size))
    return table.astype(jnp.bfloat16)


def swap_core(block, level_size):
    return lax.ppermute(block, "level", [(i, i ^ 1) for i in range(level_size)])


def from_chip(block, level_size, distance):
    return lax.ppermute(
        block, "level", [((i + 2 * distance) % level_size, i) for i in range(level_size)]
    )


def cross_pair(own_spec, other_spec):
    own = own_spec.astype(jnp.float32)
    other = other_spec.astype(jnp.float32)
    scale = 1.0 / own.shape[1]
    co_spec = (own[0] * other[0] + own[1] * other[1]).sum(axis=0) * scale
    quad_spec = (own[1] * other[0] - own[0] * other[1]).sum(axis=0) * scale
    return jnp.stack([co_spec, quad_spec])


def by_collectives(fc_long, fc_short):
    lat_local, lev_local, sample_count, var_count, lon_size = fc_long.shape
    space_size = lax.axis_size("space")
    level_size = lax.axis_size("level")
    wave_local = MK // space_size
    lat_total = lat_local * space_size
    zonal_tab = zonal_table(lon_size, MK).reshape(lon_size, 2, space_size, wave_local)
    zonal_tab = zonal_tab.transpose(0, 2, 1, 3)
    merid_tab = merid_table(lat_total, NL)
    core = lax.axis_index("level") % 2
    chip = lax.axis_index("level") // 2

    per_var = []
    for var in range(var_count):
        diff = (
            fc_long[:, 0, :, var].astype(jnp.float32) - fc_short[:, 0, :, var].astype(jnp.float32)
        ).astype(jnp.bfloat16)
        coeff = jnp.einsum(
            "ysx,xpuk->pysuk", diff, zonal_tab, preferred_element_type=jnp.float32
        ).astype(jnp.bfloat16)
        coeff = coeff.reshape(space_size * lat_local, sample_count * 2 * wave_local)
        columns = lax.all_to_all(coeff, "space", split_axis=0, concat_axis=0, tiled=True)
        products = jnp.einsum(
            "yn,ytl->ntl", columns, merid_tab, preferred_element_type=jnp.float32
        ).reshape(sample_count, 2, wave_local, 2, NL)
        real_part = products[:, 0, :, 0] + products[:, 1, :, 1]
        imag_part = products[:, 1, :, 0] - products[:, 0, :, 1]
        spectra = jnp.stack([real_part, imag_part]).astype(jnp.bfloat16)
        pairs = []
        for distance in range(level_size // 2):
            mine = spectra if distance == 0 else from_chip(spectra, level_size, distance)
            pairs.append((mine, swap_core(mine, level_size)))
        blocks = []
        for mine, mate in pairs:
            one = cross_pair(spectra, mine)
            two = cross_pair(spectra, mate)
            blocks.append(jnp.where(core == 0, one, two))
            blocks.append(jnp.where(core == 0, two, one))
        per_var.append(jnp.stack(blocks, axis=1))
    assembled = jnp.stack(per_var, axis=1)
    assembled = jnp.roll(assembled, 2 * chip, axis=2)
    return assembled[:, :, None]


LANES = 128
MESH = pl.DeviceIdType.MESH
BLOCKS = ((7, 3, 1), (0, 2, 0), (2, 2, 0), (4, 2, 0), (6, 1, 0))
HALF = len(BLOCKS)
SAMPLES = 8
IN_FLIGHT = 3


def kernel(
    space_size, lat, wave, long_hbm, short_hbm, tab_hbm, merid_hbm, merid_half_hbm, out_ref,
    long_in, short_in, tab, merid, merid_half, diff, zbuf,
    send, recv, spec, send_half, recv_half, spec_half, acc,
    in_sem, tab_sem, merid_sem,
    a2a_send, a2a_recv, own_sem, mate_send, mate_recv, far_send, far_recv, fwd_send, fwd_recv,
):
    me = lax.axis_index("space")
    level = lax.axis_index("level")
    mate = level + 1 - 2 * lax.rem(level, 2)
    far = lax.rem(level + 2, 4)
    far_mate = lax.rem(mate + 2, 4)
    rows = 2 * lat
    half = NL
    pairs = space_size // 2
    padded = recv_half.shape[0] // space_size
    own_half = pl.ds(pl.multiple_of(me * padded, 16), padded)
    own_rows = pl.ds(pl.multiple_of(me * rows, 16), rows)

    def load(var):
        return (
            pltpu.make_async_copy(long_hbm.at[:, var], long_in.at[var], in_sem.at[0, var]),
            pltpu.make_async_copy(short_hbm.at[:, var], short_in.at[var], in_sem.at[1, var]),
        )

    load_tab = pltpu.make_async_copy(tab_hbm, tab, tab_sem)
    load_merid = pltpu.make_async_copy(merid_hbm, merid, merid_sem.at[0])
    load_half = pltpu.make_async_copy(merid_half_hbm, merid_half, merid_sem.at[1])
    for copy in load(2):
        copy.start()
    load_tab.start()

    barrier = pltpu.get_barrier_semaphore()
    for d in range(1, space_size):
        peer = lax.rem(me + d, space_size)
        pl.semaphore_signal(barrier, inc=1, device_id={"space": peer}, device_id_type=MESH)
    for peer in (mate, far):
        pl.semaphore_signal(barrier, inc=1, device_id={"level": peer}, device_id_type=MESH)

    def to_peer(block, d):
        peer = lax.rem(me + d, space_size)
        if block == HALF:
            source, target = send_half.at[peer], recv_half.at[own_half]
        else:
            source, target = send[block].at[peer], recv[block].at[own_rows]
        return pltpu.make_async_remote_copy(
            src_ref=source,
            dst_ref=target,
            send_sem=a2a_send.at[block, d],
            recv_sem=a2a_recv.at[block, d],
            device_id={"space": peer},
            device_id_type=MESH,
        )

    def to_self(block):
        if block == HALF:
            return pltpu.make_async_copy(
                send_half.at[me], recv_half.at[own_half], own_sem.at[block]
            )
        return pltpu.make_async_copy(
            send[block].at[me], recv[block].at[own_rows], own_sem.at[block]
        )

    def to_level(block, peer, source, slot, send_sem, recv_sem):
        if block == HALF:
            first, second = spec_half.at[source], spec_half.at[slot]
        else:
            first, second = spec[block].at[source], spec[block].at[slot]
        return pltpu.make_async_remote_copy(
            src_ref=first,
            dst_ref=second,
            send_sem=send_sem.at[block],
            recv_sem=recv_sem.at[block],
            device_id={"level": peer},
            device_id_type=MESH,
        )

    def to_mate(block):
        return to_level(block, mate, 0, 1, mate_send, mate_recv)

    def to_far(block):
        return to_level(block, far, 0, 2, far_send, far_recv)

    def forward(block):
        return to_level(block, mate, 2, 3, fwd_send, fwd_recv)

    def difference(var):
        def part(r, carry):
            lats = pl.ds(r * 8, 8)
            delta = long_in[var, lats].astype(jnp.float32) - short_in[var, lats].astype(jnp.float32)
            delta = delta.reshape(8 * SAMPLES, delta.shape[-1]).astype(jnp.bfloat16)
            diff[var, pl.ds(pl.multiple_of(r * 8 * SAMPLES, 8 * SAMPLES), 8 * SAMPLES), :] = delta
            return carry

        lax.fori_loop(0, lat // 8, part, 0)

    def zonal(var, slot, pair):
        z = jnp.dot(diff[var], tab[pair], preferred_element_type=jnp.float32)
        zbuf[slot, 0] = z[:, :LANES]
        zbuf[slot, 1] = z[:, LANES:]

    def merged(slot0, s0, slot1, s1, j):
        lane = lax.broadcasted_iota(jnp.int32, (lat, LANES), 1)
        one = zbuf[slot0, j, pl.ds(s0, lat, stride=SAMPLES), :]
        two = zbuf[slot1, j, pl.ds(s1, lat, stride=SAMPLES), :]
        real = jnp.where(lane < wave, one, pltpu.roll(two, wave, 1))
        imag = jnp.where(lane < wave, pltpu.roll(one, LANES - wave, 1), two)
        return jnp.concatenate([real, imag], axis=0)

    def put(peer, t, tile, spread, part):
        lane = lax.broadcasted_iota(jnp.int32, (rows, LANES), 1)
        extra = pltpu.roll(spread, 2 * wave - 16 * part, 1)
        tile = jnp.where(lane < 2 * wave, tile, extra)
        for block, (first, count, _) in enumerate(BLOCKS):
            if first <= t < first + count:
                cols = slice((t - first) * LANES, (t - first + 1) * LANES)
                send[block][peer, :, cols] = tile.astype(jnp.bfloat16)

    def start_peer(block, peer):
        d = lax.rem(peer - me + space_size, space_size)

        @pl.when(peer != me)
        def _():
            to_peer(block, d).start()

    def pair_at(i):
        place = me // 2
        middle = pairs // 2
        upper = place // middle
        depth = place + upper * (pairs - 1 - 2 * place)
        order = lax.rem(i + middle * lax.rem(depth + 1, 2), pairs)
        return order + upper * (pairs - 1 - 2 * order)

    def start_block(block):
        def one_pair(i, carry):
            pair = pair_at(i)
            for j in range(2):
                start_peer(block, 2 * pair + j)
            return carry

        lax.fori_loop(0, pairs, one_pair, 0)

    def single_tiles(i, carry):
        pair = pair_at(i)
        zonal(2, 0, pair)
        lane = lax.broadcasted_iota(jnp.int32, (lat, LANES), 1)
        for j in range(2):
            peer = 2 * pair + j
            spread = merged(0, 3, 0, 7, j)
            for t in range(3):
                put(peer, 7 + t, merged(0, t, 0, t + 4, j), spread, t)
            start_peer(0, peer)
            rest = jnp.where(
                lane < 64,
                pltpu.roll(spread[:lat], LANES - 48, 1),
                pltpu.roll(spread[lat:], 64 - 48, 1),
            )
            rest = jnp.concatenate([rest, jnp.zeros((padded - lat, LANES), jnp.float32)], axis=0)
            send_half[peer] = rest.astype(jnp.bfloat16)
        return carry

    def pair_tiles(i, carry):
        pair = pair_at(i)
        zonal(0, 0, pair)
        zonal(1, 1, pair)
        for j in range(2):
            peer = 2 * pair + j
            spread = merged(0, 7, 1, 7, j)
            for t in range(7):
                put(peer, t, merged(0, t, 1, t, j), spread, t)
            start_peer(1, peer)
            start_peer(2, peer)
        return carry

    for copy in load(2):
        copy.wait()
    load_tab.wait()
    for copy in load(0) + load(1):
        copy.start()
    load_merid.start()
    load_half.start()
    difference(2)
    pl.semaphore_wait(barrier, space_size + 1)
    lax.fori_loop(0, pairs, single_tiles, 0)
    for var in (0, 1):
        for copy in load(var):
            copy.wait()
        difference(var)

    def arrive(block):
        for d in range(1, space_size):
            to_peer(block, d).wait_recv()
        if block > 0 and block + IN_FLIGHT <= HALF:
            start_block(block + IN_FLIGHT)
        to_self(block).start()
        to_self(block).wait()

    def share(block):
        to_far(block).start()
        to_mate(block).start()

    def meridional(block):
        arrive(block)

        def part(r, carry):
            r_rows = pl.ds(pl.multiple_of(r * 256, 256), 256)
            total = jnp.dot(merid[r_rows, :], recv[block][...], preferred_element_type=jnp.float32)
            spec[block][0, r_rows, :] = total.astype(jnp.bfloat16)
            return carry

        lax.fori_loop(0, 2 * half // 256, part, 0)
        share(block)

    def meridional_half():
        arrive(HALF)
        lane = lax.broadcasted_iota(jnp.int32, (half, LANES), 1)
        total = jnp.dot(merid_half[...], recv_half[...], preferred_element_type=jnp.float32)
        turned = pltpu.roll(total[half:], 64, 1)
        both = total[:half] + jnp.where(lane < 64, turned, -turned)
        spec_half[0] = both.astype(jnp.bfloat16)
        share(HALF)

    def cross_half(slot):
        step_rows = 64

        def part(r, carry):
            some = pl.ds(pl.multiple_of(r * step_rows, step_rows), step_rows)
            lane = lax.broadcasted_iota(jnp.int32, (step_rows, LANES), 1)
            here = (lane >= 48) & (lane < 48 + 64)
            a = spec_half[0, some, :].astype(jnp.float32)
            b = spec_half[slot, some, :].astype(jnp.float32)
            same = a * b
            mixed = a * pltpu.roll(b, 64, 1)
            co = same + pltpu.roll(same, 64, 1)
            quad = pltpu.roll(mixed, 64, 1) - mixed
            acc[1, 0, slot, some, :] += jnp.where(here, pltpu.roll(co, 48, 1), 0.0)
            acc[1, 1, slot, some, :] += jnp.where(here, pltpu.roll(quad, 48, 1), 0.0)
            return carry

        lax.fori_loop(0, half // step_rows, part, 0)

    def cross(block):
        first, count, group = BLOCKS[block]
        fresh = block == [g for _, _, g in BLOCKS].index(group)
        step_rows = 32

        def part(r, carry):
            base = pl.multiple_of(r * step_rows, step_rows)
            re_rows = pl.ds(base, step_rows)
            im_rows = pl.ds(pl.multiple_of(half + r * step_rows, step_rows), step_rows)
            lane = lax.broadcasted_iota(jnp.int32, (step_rows, LANES), 1)
            for slot in range(4):
                co_sum = quad_sum = None
                for i in range(count):
                    t = first + i
                    cols = slice(i * LANES, (i + 1) * LANES)
                    a_re = spec[block][0, re_rows, cols].astype(jnp.float32)
                    a_im = spec[block][0, im_rows, cols].astype(jnp.float32)
                    b_re = spec[block][slot, re_rows, cols].astype(jnp.float32)
                    b_im = spec[block][slot, im_rows, cols].astype(jnp.float32)
                    co = a_re * b_re + a_im * b_im
                    quad = a_im * b_re - a_re * b_im
                    low = 16 * (t - 7 * group)
                    here = (lane >= low) & (lane < low + 16)
                    co = co + jnp.where(here, pltpu.roll(co, low + 16, 1), 0.0)
                    quad = quad + jnp.where(here, pltpu.roll(quad, low + 16, 1), 0.0)
                    co_sum = co if co_sum is None else co_sum + co
                    quad_sum = quad if quad_sum is None else quad_sum + quad
                if fresh:
                    acc[group, 0, slot, re_rows, :] = co_sum
                    acc[group, 1, slot, re_rows, :] = quad_sum
                else:
                    acc[group, 0, slot, re_rows, :] += co_sum
                    acc[group, 1, slot, re_rows, :] += quad_sum
            return carry

        lax.fori_loop(0, half // step_rows, part, 0)

    scale = 1.0 / SAMPLES

    def write(slot, b):
        for c in range(2):
            pair = acc[0, c, slot].T * scale
            single = acc[1, c, slot].T * scale
            out_ref[c, 0, b] = pair[:wave]
            out_ref[c, 1, b] = pair[wave : 2 * wave]
            out_ref[c, 2, b] = single[:wave] + single[wave : 2 * wave]

    def relay(block):
        to_far(block).wait_recv()
        forward(block).start()

    def finish(block):
        to_mate(block).wait_recv()
        forward(block).wait_recv()
        cross(block)

    lax.fori_loop(0, pairs // 2, pair_tiles, 0)
    load_merid.wait()
    load_half.wait()
    meridional(0)
    lax.fori_loop(pairs // 2, pairs, pair_tiles, 0)
    start_block(IN_FLIGHT)
    for block in range(1, HALF):
        meridional(block)
        relay(block - 1)
        if block >= 2:
            finish(block - 2)
    finish(HALF - 2)
    relay(HALF - 1)
    meridional_half()
    finish(HALF - 1)
    cross_half(0)
    write(0, level)
    to_mate(HALF).wait_recv()
    cross_half(1)
    relay(HALF)
    write(1, mate)
    cross_half(2)
    write(2, far)
    forward(HALF).wait_recv()
    cross_half(3)
    write(3, far_mate)

    for block in range(HALF + 1):
        for d in range(1, space_size):
            to_peer(block, d).wait_send()
        to_mate(block).wait_send()
        to_far(block).wait_send()
        forward(block).wait_send()


def by_kernel(fc_long, fc_short):
    lat, lev_local, sample_count, var_count, lon_size = fc_long.shape
    space_size = lax.axis_size("space")
    wave = MK // space_size
    pairs = space_size // 2
    rows = 2 * lat
    bf16 = jnp.bfloat16
    table = zonal_table(lon_size, MK).reshape(lon_size, 2, pairs, 2, wave).transpose(2, 0, 3, 1, 4)
    padded = np.zeros((pairs, lon_size, 2, LANES), jnp.bfloat16)
    padded[..., : 2 * wave] = table.reshape(pairs, lon_size, 2, 2 * wave)
    padded = padded.reshape(pairs, lon_size, 2 * LANES)
    merid = merid_table(lat * space_size, NL).reshape(space_size, lat, 2, NL)
    cos, sin = merid[:, :, 0], merid[:, :, 1]
    stacked = np.stack([np.stack([cos, sin], axis=1), np.stack([-sin, cos], axis=1)])
    stacked = stacked.transpose(0, 4, 1, 2, 3).reshape(2 * NL, space_size * rows)
    row_pad = -(-lat // 16) * 16
    halves = np.zeros((2, NL, space_size, row_pad), bf16)
    halves[..., :lat] = np.stack([cos, sin]).transpose(0, 3, 1, 2)
    halves = halves.reshape(2 * NL, space_size * row_pad)
    blocks = HALF + 1
    widths = [count * LANES for _, count, _ in BLOCKS]
    sems = pltpu.SemaphoreType.DMA
    out = pl.pallas_call(
        functools.partial(kernel, space_size, lat, wave),
        out_shape=jax.ShapeDtypeStruct((2, var_count, 4, wave, NL), jnp.float32),
        in_specs=[pl.BlockSpec(memory_space=pl.ANY)] * 5,
        out_specs=pl.BlockSpec(memory_space=pltpu.VMEM),
        scratch_shapes=[
            pltpu.VMEM((var_count, lat, sample_count, lon_size), bf16),
            pltpu.VMEM((var_count, lat, sample_count, lon_size), bf16),
            pltpu.VMEM(padded.shape, bf16),
            pltpu.VMEM(stacked.shape, bf16),
            pltpu.VMEM(halves.shape, bf16),
            pltpu.VMEM((var_count, lat * sample_count, lon_size), bf16),
            pltpu.VMEM((2, 2, lat * sample_count, LANES), jnp.float32),
            [pltpu.VMEM((space_size, rows, width), bf16) for width in widths],
            [pltpu.VMEM((space_size * rows, width), bf16) for width in widths],
            [pltpu.VMEM((4, 2 * NL, width), bf16) for width in widths],
            pltpu.VMEM((space_size, row_pad, LANES), bf16),
            pltpu.VMEM((space_size * row_pad, LANES), bf16),
            pltpu.VMEM((4, NL, LANES), bf16),
            pltpu.VMEM((2, 2, 4, NL, LANES), jnp.float32),
            sems((2, var_count)),
            sems,
            sems((2,)),
            sems((blocks, space_size)),
            sems((blocks, space_size)),
        ]
        + [sems((blocks,))] * 7,
        compiler_params=pltpu.CompilerParams(
            collective_id=0, has_side_effects=True, vmem_limit_bytes=58 * 1024 * 1024
        ),
    )(
        fc_long[:, 0].transpose(0, 2, 1, 3),
        fc_short[:, 0].transpose(0, 2, 1, 3),
        jnp.asarray(padded),
        jnp.asarray(stacked),
        jnp.asarray(halves),
    )
    return out[:, :, None]


def on_device(fc_long, fc_short):
    lat, lev_local, sample_count, var_count, lon_size = fc_long.shape
    space_size = lax.axis_size("space")
    fits = (
        lat % 8 == 0
        and 2 * (MK // space_size) == LANES - 16
        and (lev_local, sample_count, var_count) == (1, SAMPLES, 3)
        and space_size % 4 == 0
        and lax.axis_size("level") == 4
        and 2 * NL % 256 == 0
    )
    return by_kernel(fc_long, fc_short) if fits else by_collectives(fc_long, fc_short)


def solution(mesh):
    placed = (P("space", "level", None, None, None), P("space", "level", None, None, None))
    return jax.shard_map(
        on_device,
        mesh=mesh,
        in_specs=placed,
        out_specs=P(None, None, "level", None, "space", None),
        check_vma=False,
    )
```
